512 devices in a mesh: gx: 8 (over z), gy: 16 (over y_lo, x), gz: 4 (over y_hi, core).
Axes of the slice: x: 4, y: 8 (y_hi: 2, y_lo: 4; y = y_hi * 4 + y_lo), z: 8, core: 2. Of those that a mesh axis runs over, the one named last changes fastest.
Arguments:
- q_dagger: float32 [64, 128, 32, 512], P(None, 'gy', 'gx', 'gz'), may hold values from 0.2 to 3
- forward: float32 [2, 64, 128, 32, 512], P(None, None, 'gy', 'gx', 'gz'), may hold values from 0.2 to 2
- field_iso: float32 [128, 32, 512], P('gy', 'gx', 'gz'), may hold values from -6 to 6
- field_order: float32 [3, 128, 32, 512], P(None, 'gy', 'gx', 'gz'), may hold values from -6 to 6
- sphere_step: float32 [64, 64], replicated, may hold values from -0.75 to 0.75
- upwind_sign: int32 [3, 64], replicated, may hold values from 0 to 1, as said below
- direction_size: float32 [3, 64], replicated, may hold values from 0.1 to 1
- sphere_weight: float32 [64], replicated, may hold values from 0.05 to 0.3
Outputs:
- q_final: float32 [64, 128, 32, 512], P(None, 'gy', 'gx', 'gz')
- density: float32 [128, 32, 512], P('gy', 'gx', 'gz')
- order_density: float32 [3, 128, 32, 512], P(None, 'gy', 'gx', 'gz')
The draws below stay inside these ranges and needn't reach their ends.
Inputs may be any that keep to these rules, and one draw needn't show every extreme that they name: `upwind_sign`: 1 marks an orientation whose upwind neighbour along that axis lies at the higher index, 0 at the lower; along each axis exactly 32 orientations are 1.
All inputs are finite; a program needn't handle non-finite values.
Results may differ from the reference program's by a relative error of at most 0.00017.
Values sent between devices are 32-bit elements; how exact they have to be, the bound alone decides.
A program may use at most 64 MiB of HBM per device.

```python
import math
import jax
import jax.numpy as jnp
from jax import lax

U = 64
STEPS = 2
NX = 128
NY = 32
NZ = 512


def draw_upwind_sign(key, part):
    key = jax.random.fold_in(key, 7)
    rows = []
    for direction_axis in range(3):
        shuffled = jax.random.permutation(jax.random.fold_in(key, direction_axis), U)
        rows.append((shuffled < U // 2).astype(jnp.int32))
    return jnp.stack(rows, axis=0)


def levels(rng, dims, cuts, smallest, top_value):
    loudness, own = 1.0, jax.random.fold_in(rng, 6)
    for axis_at, blocks in cuts:
        draws = jnp.exp(jax.random.uniform(jax.random.fold_in(own, axis_at), (blocks,), jnp.float32, smallest / len(cuts), top_value / len(cuts)))
        loudness = loudness * jnp.repeat(draws, dims[axis_at] // blocks).reshape([-1 if axis == axis_at else 1 for axis in range(len(dims))])
    return loudness


def gaussian(stream_key, shape, scale, limit, split=(), kind=jnp.bfloat16):
    array = jax.random.normal(stream_key, shape, jnp.float32) * scale
    if len(split) > 0:
        array = levels(stream_key, shape, split, -0.22, 0.18) * array
    return jnp.clip(array, min=-limit, max=limit).astype(kind)


def setup_inputs(seed: int = 0) -> dict:
    seeds = jax.random.split(jax.random.key(seed), 9)
    return {
        "q_dagger": jnp.clip(jnp.exp(math.log(3.0) - 2.7080502 * jax.random.uniform(seeds[0], (U, NX, NY, NZ), jnp.float32) ** levels(seeds[0], (U, NX, NY, NZ), ((1, 16), (2, 8), (3, 4)), -0.2, 0.2)), 0.2, 3.0),
        "forward": jnp.clip(0.2 + 1.8 * jax.random.uniform(seeds[1], (STEPS, U, NX, NY, NZ), jnp.float32) ** levels(seeds[1], (STEPS, U, NX, NY, NZ), ((2, 16), (3, 8), (4, 4)), -0.2, 0.2), 0.2, 2.0),
        "field_iso": gaussian(seeds[2], (NX, NY, NZ), 1.0, 6.0, ((0, 16), (1, 8), (2, 4)), jnp.float32),
        "field_order": gaussian(seeds[3], (3, NX, NY, NZ), 1.5, 6.0, ((1, 16), (2, 8), (3, 4)), jnp.float32),
        "sphere_step": gaussian(seeds[4], (U, U), U ** -0.5, 0.75, (), jnp.float32),
        "upwind_sign": draw_upwind_sign(jax.random.fold_in(seeds[8], 71), 0),
        "direction_size": jnp.clip(jax.random.uniform(seeds[6], (3, U), jnp.float32, 0.1, 1.0), 0.1, 1.0),
        "sphere_weight": jnp.clip(jnp.exp(jax.random.uniform(seeds[7], (U,), jnp.float32, math.log(0.05), math.log(0.3))), 0.05, 0.3),
    }


SPEED = 0.5
HALF_DOSE = 0.2

def directions(upwind_sign, direction_size):
    signed = (2 * upwind_sign - 1).astype(jnp.float32) * direction_size
    length = jnp.sqrt(lax.optimization_barrier(jnp.sum(signed * signed, axis=0)))
    return signed / length

def exponent_factor(field_iso, field_order, shape_terms):
    field = field_iso[None] + jnp.einsum('au,axyz->uxyz', shape_terms, field_order, precision=lax.Precision.HIGHEST)
    return jnp.exp(-HALF_DOSE * field)

def advect(padded, along, upwind_sign):
    center = padded[:, 1:-1, 1:-1, 1:-1]
    uppers = (padded[:, 2:, 1:-1, 1:-1], padded[:, 1:-1, 2:, 1:-1], padded[:, 1:-1, 1:-1, 2:])
    lowers = (padded[:, :-2, 1:-1, 1:-1], padded[:, 1:-1, :-2, 1:-1], padded[:, 1:-1, 1:-1, :-2])
    moved = center
    for direction_axis in range(3):
        upper_side = (upwind_sign[direction_axis] == 1)[:, None, None, None]
        speeds = jnp.abs(along[direction_axis])[:, None, None, None]
        chosen = jnp.where(upper_side, uppers[direction_axis], lowers[direction_axis])
        moved = moved + SPEED * speeds * (chosen - center)
    return moved

def sphere_mix(values, sphere_step):
    flat = values.reshape(values.shape[0], -1)
    mixed = jnp.dot(sphere_step, flat, precision=lax.Precision.HIGHEST, preferred_element_type=jnp.float32)
    return mixed.reshape(values.shape)

def reference(q_dagger, forward, field_iso, field_order, sphere_step, upwind_sign, direction_size, sphere_weight):
    along = directions(upwind_sign, direction_size)
    shape_terms = along * along - 1.0 / 3.0
    factor = exponent_factor(field_iso, field_order, shape_terms)
    current = q_dagger
    density = jnp.zeros(field_iso.shape, jnp.float32)
    order_density = jnp.zeros(field_order.shape, jnp.float32)
    for contour in range(STEPS):
        weighted = factor * current
        padded = jnp.pad(weighted, ((0, 0), (1, 1), (1, 1), (1, 1)), mode='wrap')
        current = factor * sphere_mix(advect(padded, along, upwind_sign), sphere_step)
        product = sphere_weight[:, None, None, None] * forward[contour] * current
        density = density + lax.optimization_barrier(jnp.sum(product, axis=0)) / STEPS
        order_density = order_density + jnp.einsum('au,uxyz->axyz', shape_terms, product, precision=lax.Precision.HIGHEST) / STEPS
    return (current, density, order_density)
```

```python
import functools
import math

import jax
import jax.numpy as jnp
from jax import lax
from jax.experimental import pallas as pl
from jax.experimental.pallas import tpu as pltpu
from jax.sharding import PartitionSpec as P

U = 64
HALF = U // 2
LANES = 128
X = 8
Y = 4
ROWS = X * Y
STEPS = 2
RATE = -0.2 / math.log(2.0)
F32 = jnp.float32
BF16 = jnp.bfloat16

UP_X, LOW_X, UP_Y, LOW_Y, SPEED_Z, KEEP, SHAPE_0, SHAPE_1, SHAPE_2, SIGN_Z, RANK_X, RANK_Y = range(12)


def split(values):
    high = values.astype(BF16)
    low = (values - high.astype(F32)).astype(BF16)
    return high, low


def iota(shape, dim):
    return lax.broadcasted_iota(jnp.int32, shape, dim)


def neighbour(axis, step):
    count = lax.axis_size(axis)
    return {axis: lax.rem(lax.axis_index(axis) + count + step, count)}


def kernel(
    q_hbm, forward_hbm, iso_hbm, order_hbm, sphere_hbm, sign_hbm, size_hbm, weight_hbm,
    out_q, out_density, out_order,
    q, forward, factor, field, order, sphere, sign, size, weight,
    cells, coef, table, mix4, sum4, pack, unpack,
    send_x, send_y, send_z, recv_x, recv_y, recv_z, dens,
    load_sem, q_sem, forward_sem, store_sem, send_sem, recv_sem,
):
    sides = [("gx", 1), ("gx", -1), ("gy", 1), ("gy", -1), ("gz", 1), ("gz", -1)]
    barrier = pltpu.get_barrier_semaphore()
    for axis, step in sides:
        pl.semaphore_signal(
            barrier, inc=1, device_id=neighbour(axis, step), device_id_type=pl.DeviceIdType.MESH
        )

    small = [
        pltpu.make_async_copy(src, dst, load_sem.at[n])
        for n, (src, dst) in enumerate(
            [(sign_hbm, sign), (size_hbm, size), (weight_hbm, weight), (sphere_hbm, sphere),
             (iso_hbm, field), (order_hbm, order)]
        )
    ]
    for copy in small:
        copy.start()

    def load_q(row, carry):
        pltpu.make_async_copy(q_hbm.at[:, row, 0, :], q.at[row], q_sem.at[0]).start()
        return carry

    lax.fori_loop(0, ROWS, load_q, 0)

    def load_forward(row, carry):
        for step in range(STEPS):
            pltpu.make_async_copy(
                forward_hbm.at[step, :, row, 0, :], forward.at[step, row], forward_sem.at[step]
            ).start()
        return carry

    lax.fori_loop(0, ROWS, load_forward, 0)

    for copy in small:
        copy.wait()
    signs = sign[...].astype(F32)
    signed = (2.0 * signs - 1.0) * size[...]
    length = jnp.sqrt(jnp.sum(signed * signed, axis=0, keepdims=True))
    along = signed / length
    shape = along * along - 1.0 / 3.0
    speed = 0.5 * jnp.abs(along)
    below = (iota((U, U), 0) < iota((U, U), 1)).astype(BF16)
    ones_before = jnp.dot(signs.astype(BF16), below, preferred_element_type=F32)
    place = iota((1, U), 1).astype(F32)
    rank = jnp.where(signs > 0.5, ones_before, HALF + place - ones_before)
    keep = 1.0 - jnp.sum(speed, axis=0, keepdims=True)
    upper = speed * signs
    lower = speed * (1.0 - signs)
    rows = [
        upper[0:1], lower[0:1], upper[1:2], lower[1:2], speed[2:3], keep,
        RATE * shape[0:1], RATE * shape[1:2], RATE * shape[2:3],
        signs[2:3], rank[0:1], rank[1:2],
    ]
    stacked = jnp.zeros((16, U), F32)
    which = iota((16, U), 0)
    for n, row in enumerate(rows):
        stacked = jnp.where(which == n, row, stacked)
    table[...] = jnp.zeros((LANES, LANES), F32)
    table[0:16, 0:U] = stacked
    columns = jnp.transpose(table[...])
    for n in range(10):
        coef[n] = jnp.broadcast_to(columns[0:U, n : n + 1], (U, LANES))
    half_weight = weight[...] / STEPS
    sums = jnp.zeros((16, U), F32)
    for n, row in enumerate(
        [half_weight, half_weight * shape[0:1], half_weight * shape[1:2], half_weight * shape[2:3]]
    ):
        sums = jnp.where(which == n, row, sums)
    high, low = split(sums)
    sum4[...] = jnp.concatenate([high, high, low, low], axis=1)
    high, low = split(sphere[...])
    mix4[...] = jnp.concatenate([high, high, low, low], axis=1)
    for axis in range(2):
        to_rank = (iota((U, U), 0).astype(F32) == rank[axis : axis + 1]).astype(BF16)
        pack[axis] = jnp.concatenate([to_rank, to_rank], axis=1)
        from_rank = (
            iota((U, LANES), 1).astype(F32) == columns[0:U, RANK_X + axis : RANK_X + axis + 1]
        ) | (
            (iota((U, LANES), 1) - U).astype(F32) == columns[0:U, RANK_X + axis : RANK_X + axis + 1]
        )
        unpack[axis] = from_rank.astype(BF16)

    lane = iota((16, LANES), 1)

    pltpu.make_async_copy(q, q, q_sem.at[0]).wait()

    def start(x, carry):
        for group in range(4):
            part = pl.ds(16 * group, 16)
            shapes = [coef[SHAPE_0 + n, part, :] for n in range(3)]
            for y in range(Y):
                exponent = RATE * field[x, y : y + 1, :]
                for n in range(3):
                    exponent = exponent + shapes[n] * order[n, x, y : y + 1, :]
                value = jnp.exp2(exponent)
                factor[Y * x + y, part, :] = value
                cells[0, x + 1, y + 1, part, :] = value * q[Y * x + y, part, :]
        return carry

    lax.fori_loop(0, X, start, 0)

    for step in range(STEPS):
        zeros = jnp.zeros((16, LANES), F32)

        def edges(x, carry):
            out = list(carry)
            for group in range(4):
                part = pl.ds(16 * group, 16)
                for y in range(Y):
                    to = 64 * (group // 2) + 2 * (Y * x + y)
                    turned = pltpu.roll(cells[step, x + 1, y + 1, part, :], to, 1)
                    chosen = (lane == to) | (lane == lax.rem(to + 127, 128))
                    out[group % 2] = jnp.where(chosen, turned, out[group % 2])
            return tuple(out)

        first, second = lax.fori_loop(0, X, edges, (zeros, zeros))
        send_z[step, 0:16, :] = first
        send_z[step, 16:32, :] = second

        def face_y(x, carry):
            faces = jnp.concatenate([cells[step, x + 1, 1], cells[step, x + 1, Y]], axis=1)
            packed = jnp.dot(
                pack[1], jnp.concatenate(split(faces), axis=0), preferred_element_type=F32
            )
            send_y[step, 0, x] = packed[0:HALF, 0:LANES]
            send_y[step, 1, x] = packed[HALF:U, LANES : 2 * LANES]
            return carry

        lax.fori_loop(0, X, face_y, 0)
        for y in range(Y):
            faces = jnp.concatenate([cells[step, 1, y + 1], cells[step, X, y + 1]], axis=1)
            packed = jnp.dot(
                pack[0], jnp.concatenate(split(faces), axis=0), preferred_element_type=F32
            )
            send_x[step, 0, y] = packed[0:HALF, 0:LANES]
            send_x[step, 1, y] = packed[HALF:U, LANES : 2 * LANES]

        if step == 0:
            pl.semaphore_wait(barrier, 6)
        copies = []
        for n, (src, dst, axis, way) in enumerate(
            [
                (send_z.at[step], recv_z.at[step, 0], "gz", -1),
                (send_z.at[step], recv_z.at[step, 1], "gz", 1),
                (send_y.at[step, 0], recv_y.at[step, :, 0:HALF, :], "gx", -1),
                (send_y.at[step, 1], recv_y.at[step, :, HALF:U, :], "gx", 1),
                (send_x.at[step, 0], recv_x.at[step, :, 0:HALF, :], "gy", -1),
                (send_x.at[step, 1], recv_x.at[step, :, HALF:U, :], "gy", 1),
            ]
        ):
            copy = pltpu.make_async_remote_copy(
                src_ref=src, dst_ref=dst, send_sem=send_sem.at[step, n], recv_sem=recv_sem.at[step, n],
                device_id=neighbour(axis, way), device_id_type=pl.DeviceIdType.MESH,
            )
            copy.start()
            copies.append(copy)
        for copy in copies:
            copy.wait()

        def place_y(n, carry):
            received = jnp.concatenate([recv_y[step, 2 * n], recv_y[step, 2 * n + 1]], axis=1)
            chosen = jnp.dot(
                unpack[1], jnp.concatenate(split(received), axis=0), preferred_element_type=F32
            )
            for side in (0, Y + 1):
                cells[step, 2 * n + 1, side] = chosen[:, 0:LANES]
                cells[step, 2 * n + 2, side] = chosen[:, LANES : 2 * LANES]
            return carry

        lax.fori_loop(0, X // 2, place_y, 0)
        for y in range(0, Y, 2):
            received = jnp.concatenate([recv_x[step, y], recv_x[step, y + 1]], axis=1)
            chosen = jnp.dot(
                unpack[0], jnp.concatenate(split(received), axis=0), preferred_element_type=F32
            )
            for side in (0, X + 1):
                cells[step, side, y + 1] = chosen[:, 0:LANES]
                cells[step, side, y + 2] = chosen[:, LANES : 2 * LANES]

        ends = []
        for n in range(2):
            part = pl.ds(16 * n, 16)
            ends.append(
                jnp.where(
                    lax.rem(lane, 2) == 0,
                    recv_z[step, 0, part, :],
                    pltpu.roll(recv_z[step, 1, part, :], 2, 1),
                )
            )
        pltpu.make_async_copy(forward.at[step], forward.at[step], forward_sem.at[step]).wait()

        def advance(x, carry):
            parts = [([], []) for _ in range(Y)]
            for group in range(4):
                part = pl.ds(16 * group, 16)
                up_x, low_x, up_y, low_y, speed_z, kept = [coef[n, part, :] for n in range(6)]
                up_z = coef[SIGN_Z, part, :] > 0.5
                edge = ((lane == 127) & up_z) | ((lane == 0) & ~up_z)
                for y in range(Y):
                    here = cells[step, x + 1, y + 1, part, :]
                    beside = jnp.where(up_z, pltpu.roll(here, 127, 1), pltpu.roll(here, 1, 1))
                    to = lax.rem(255 - 64 * (group // 2) - 2 * (Y * x + y), 128)
                    beside = jnp.where(edge, pltpu.roll(ends[group % 2], to, 1), beside)
                    moved = (
                        kept * here
                        + up_x * cells[step, x + 2, y + 1, part, :]
                        + low_x * cells[step, x, y + 1, part, :]
                        + up_y * cells[step, x + 1, y + 2, part, :]
                        + low_y * cells[step, x + 1, y, part, :]
                        + speed_z * beside
                    )
                    high, low = split(moved)
                    parts[y][0].append(high)
                    parts[y][1].append(low)
            for y in range(0, Y, 2):
                stack = [jnp.concatenate(parts[n][0] + parts[n][1], axis=0) for n in (y, y + 1)]
                stack = jnp.concatenate(stack, axis=1)
                mixed = jnp.dot(
                    mix4[...], jnp.concatenate([stack, stack], axis=0), preferred_element_type=F32
                )
                sums = []
                for n in range(2):
                    row = Y * x + y + n
                    value = factor[row] * mixed[:, LANES * n : LANES * (n + 1)]
                    if step == 0:
                        cells[1, x + 1, y + n + 1] = factor[row] * value
                        forward[0, row] = forward[0, row] * value
                    else:
                        q[row] = value
                        total = forward[0, row] + forward[1, row] * value
                        sums.append(jnp.concatenate(split(total), axis=0))
                        pltpu.make_async_copy(
                            q.at[row], out_q.at[:, row, 0, :], store_sem.at[0]
                        ).start()
                if step == 1:
                    sums = jnp.concatenate(sums, axis=1)
                    summed = jnp.dot(
                        sum4[...], jnp.concatenate([sums, sums], axis=0), preferred_element_type=F32
                    )
                    for n in range(2):
                        for a in range(4):
                            dens[a, x, y + n : y + n + 1, :] = summed[
                                a : a + 1, LANES * n : LANES * (n + 1)
                            ]
            return carry

        lax.fori_loop(0, X, advance, 0)

    last = [
        pltpu.make_async_copy(dens.at[0], out_density, store_sem.at[1]),
        pltpu.make_async_copy(dens.at[1:4], out_order, store_sem.at[2]),
    ]
    for copy in last:
        copy.start()
    for copy in last:
        copy.wait()
    pltpu.make_async_copy(q, q, store_sem.at[0]).wait()


def body(q_dagger, forward, field_iso, field_order, sphere_step, upwind_sign, direction_size, sphere_weight):
    anywhere = pl.BlockSpec(memory_space=pl.ANY)
    cells = (U, ROWS, 1, LANES)
    q, density, order = pl.pallas_call(
        kernel,
        out_shape=(
            jax.ShapeDtypeStruct(cells, F32),
            jax.ShapeDtypeStruct(field_iso.shape, F32),
            jax.ShapeDtypeStruct(field_order.shape, F32),
        ),
        in_specs=[anywhere] * 8,
        out_specs=(anywhere,) * 3,
        scratch_shapes=[
            pltpu.VMEM((ROWS, U, LANES), F32),
            pltpu.VMEM((STEPS, ROWS, U, LANES), F32),
            pltpu.VMEM((ROWS, U, LANES), F32),
            pltpu.VMEM((X, Y, LANES), F32),
            pltpu.VMEM((3, X, Y, LANES), F32),
            pltpu.VMEM((U, U), F32),
            pltpu.VMEM((3, U), jnp.int32),
            pltpu.VMEM((3, U), F32),
            pltpu.VMEM((1, U), F32),
            pltpu.VMEM((STEPS, X + 2, Y + 2, U, LANES), F32),
            pltpu.VMEM((10, U, LANES), F32),
            pltpu.VMEM((LANES, LANES), F32),
            pltpu.VMEM((U, 4 * U), BF16),
            pltpu.VMEM((16, 4 * U), BF16),
            pltpu.VMEM((2, U, 2 * U), BF16),
            pltpu.VMEM((2, U, 2 * U), BF16),
            pltpu.VMEM((STEPS, 2, Y, HALF, LANES), F32),
            pltpu.VMEM((STEPS, 2, X, HALF, LANES), F32),
            pltpu.VMEM((STEPS, HALF, LANES), F32),
            pltpu.VMEM((STEPS, Y, U, LANES), F32),
            pltpu.VMEM((STEPS, X, U, LANES), F32),
            pltpu.VMEM((STEPS, 2, HALF, LANES), F32),
            pltpu.VMEM((4, X, Y, LANES), F32),
            pltpu.SemaphoreType.DMA((6,)),
            pltpu.SemaphoreType.DMA((1,)),
            pltpu.SemaphoreType.DMA((STEPS,)),
            pltpu.SemaphoreType.DMA((3,)),
            pltpu.SemaphoreType.DMA((STEPS, 6)),
            pltpu.SemaphoreType.DMA((STEPS, 6)),
        ],
        compiler_params=pltpu.CompilerParams(
            collective_id=0, has_side_effects=True, vmem_limit_bytes=48 * 1024 * 1024
        ),
        name="propagate",
    )(
        q_dagger.reshape(cells), forward.reshape((STEPS,) + cells), field_iso, field_order,
        sphere_step, upwind_sign, direction_size, sphere_weight.reshape(1, U),
    )
    return q.reshape(q_dagger.shape), density, order


def solution(mesh):
    grid = P("gy", "gx", "gz")
    placed = (
        P(None, "gy", "gx", "gz"), P(None, None, "gy", "gx", "gz"), grid,
        P(None, "gy", "gx", "gz"), P(), P(), P(), P(),
    )
    return jax.shard_map(
        body, mesh=mesh, in_specs=placed,
        out_specs=(P(None, "gy", "gx", "gz"), grid, P(None, "gy", "gx", "gz")), check_vma=False,
    )
```

```python
import functools
import math

import jax
import jax.numpy as jnp
from jax import lax
from jax.experimental import pallas as pl
from jax.experimental.pallas import tpu as pltpu
from jax.sharding import PartitionSpec as P

U = 64
HALF = U // 2
LANES = 128
X = 8
Y = 4
ROWS = X * Y
STEPS = 2
RATE = -0.2 / math.log(2.0)
F32 = jnp.float32
BF16 = jnp.bfloat16

UP_X, LOW_X, UP_Y, LOW_Y, SPEED_Z, KEEP, SHAPE_0, SHAPE_1, SHAPE_2, SIGN_Z, RANK_X, RANK_Y = range(12)


def split(values):
    high = values.astype(BF16)
    low = (values - high.astype(F32)).astype(BF16)
    return high, low


def iota(shape, dim):
    return lax.broadcasted_iota(jnp.int32, shape, dim)


def neighbour(axis, step):
    count = lax.axis_size(axis)
    return {axis: lax.rem(lax.axis_index(axis) + count + step, count)}


def advance(
    step, x, cells, factor, coef, mix4, ends, forward, total, nxt=None, sum4=None, q=None, dens=None
):
    lane = iota((16, LANES), 1)
    parts = [([], []) for _ in range(Y)]
    for group in range(4):
        part = pl.ds(16 * group, 16)
        up_x, low_x, up_y, low_y, speed_z, kept = [coef[n, part, :] for n in range(6)]
        up_z = coef[SIGN_Z, part, :] > 0.5
        edge = ((lane == 127) & up_z) | ((lane == 0) & ~up_z)
        for y in range(Y):
            here = cells[x + 1, y + 1, part, :]
            beside = jnp.where(up_z, pltpu.roll(here, 127, 1), pltpu.roll(here, 1, 1))
            to = (255 - 64 * (group // 2) - 2 * (Y * x + y)) % 128
            beside = jnp.where(edge, pltpu.roll(ends[group % 2], to, 1), beside)
            moved = (
                kept * here
                + up_x * cells[x + 2, y + 1, part, :]
                + low_x * cells[x, y + 1, part, :]
                + up_y * cells[x + 1, y + 2, part, :]
                + low_y * cells[x + 1, y, part, :]
                + speed_z * beside
            )
            high, low = split(moved)
            parts[y][0].append(high)
            parts[y][1].append(low)
    for y in range(0, Y, 2):
        stack = [jnp.concatenate(parts[n][0] + parts[n][1], axis=0) for n in (y, y + 1)]
        stack = jnp.concatenate(stack, axis=1)
        mixed = jnp.dot(
            mix4[...], jnp.concatenate([stack, stack], axis=0), preferred_element_type=F32
        )
        sums = []
        for n in range(2):
            row = Y * x + y + n
            value = factor[row] * mixed[:, LANES * n : LANES * (n + 1)]
            if step == 0:
                nxt[x + 1, y + n + 1] = factor[row] * value
                total[row] = forward[row] * value
            else:
                q[row] = value
                sums.append(jnp.concatenate(split(total[row] + forward[row] * value), axis=0))
        if step == 1:
            sums = jnp.concatenate(sums, axis=1)
            summed = jnp.dot(
                sum4[...], jnp.concatenate([sums, sums], axis=0), preferred_element_type=F32
            )
            for n in range(2):
                for a in range(4):
                    dens[a, x, y + n : y + n + 1, :] = summed[
                        a : a + 1, LANES * n : LANES * (n + 1)
                    ]


def z_ends(recv, slot=None):
    lane = iota((16, LANES), 1)
    ends = []
    for n in range(2):
        part = pl.ds(16 * n, 16)
        ends.append(
            jnp.where(
                lax.rem(lane, 2) == 0, recv[0, part, :], pltpu.roll(recv[1, part, :], 2, 1)
            )
        )
    return ends


def finish(
    cells, factor, total, forward, coef, mix4, sum4, ends,
    out_q, out_density, out_order, q, dens, store_sem,
):
    copies = []
    edge = [ends[0:16, :], ends[16:32, :]]
    for x in range(X):
        advance(1, x, cells, factor, coef, mix4, edge, forward, total, sum4=sum4, q=q, dens=dens)
        for row in range(Y * x, Y * x + Y):
            copy = pltpu.make_async_copy(q.at[row], out_q.at[:, row, 0, :], store_sem.at[row])
            copy.start()
            copies.append(copy)
    for copy in (
        pltpu.make_async_copy(dens.at[0], out_density, store_sem.at[ROWS]),
        pltpu.make_async_copy(dens.at[1:4], out_order, store_sem.at[ROWS + 1]),
    ):
        copy.start()
        copies.append(copy)
    for copy in copies:
        copy.wait()


def kernel(
    q_hbm, forward_hbm, iso_hbm, order_hbm, sphere_hbm, sign_hbm, size_hbm, weight_hbm,
    nxt, factor, total, forward_1, coef, mix4, sum4, ends_out,
    q, forward_0, field, order, sphere, sign, size, weight,
    first, table, pack, unpack,
    send_x, send_y, send_z, recv_x, recv_y, recv_z,
    load_sem, q_sem, forward_sem, send_sem, recv_sem,
):
    forward = (forward_0, forward_1)
    grids = (first, nxt)
    sides = [("gx", 1), ("gx", -1), ("gy", 1), ("gy", -1), ("gz", 1), ("gz", -1)]
    barrier = pltpu.get_barrier_semaphore()
    for axis, step in sides:
        pl.semaphore_signal(
            barrier, inc=1, device_id=neighbour(axis, step), device_id_type=pl.DeviceIdType.MESH
        )

    small = [
        pltpu.make_async_copy(src, dst, load_sem.at[n])
        for n, (src, dst) in enumerate(
            [(sign_hbm, sign), (size_hbm, size), (weight_hbm, weight), (sphere_hbm, sphere),
             (iso_hbm, field), (order_hbm, order)]
        )
    ]
    for copy in small:
        copy.start()

    def load_q(row, carry):
        pltpu.make_async_copy(q_hbm.at[:, row, 0, :], q.at[row], q_sem.at[0]).start()
        return carry

    lax.fori_loop(0, ROWS, load_q, 0)

    def load_forward(row, carry):
        for step in range(STEPS):
            pltpu.make_async_copy(
                forward_hbm.at[step, :, row, 0, :], forward[step].at[row], forward_sem.at[step]
            ).start()
        return carry

    lax.fori_loop(0, ROWS, load_forward, 0)

    for copy in small:
        copy.wait()
    signs = sign[...].astype(F32)
    signed = (2.0 * signs - 1.0) * size[...]
    length = jnp.sqrt(jnp.sum(signed * signed, axis=0, keepdims=True))
    along = signed / length
    shape = along * along - 1.0 / 3.0
    speed = 0.5 * jnp.abs(along)
    below = (iota((U, U), 0) < iota((U, U), 1)).astype(BF16)
    ones_before = jnp.dot(signs.astype(BF16), below, preferred_element_type=F32)
    place = iota((1, U), 1).astype(F32)
    rank = jnp.where(signs > 0.5, ones_before, HALF + place - ones_before)
    keep = 1.0 - jnp.sum(speed, axis=0, keepdims=True)
    upper = speed * signs
    lower = speed * (1.0 - signs)
    rows = [
        upper[0:1], lower[0:1], upper[1:2], lower[1:2], speed[2:3], keep,
        RATE * shape[0:1], RATE * shape[1:2], RATE * shape[2:3],
        signs[2:3], rank[0:1], rank[1:2],
    ]
    stacked = jnp.zeros((16, U), F32)
    which = iota((16, U), 0)
    for n, row in enumerate(rows):
        stacked = jnp.where(which == n, row, stacked)
    table[...] = jnp.zeros((LANES, LANES), F32)
    table[0:16, 0:U] = stacked
    columns = jnp.transpose(table[...])
    for n in range(10):
        coef[n] = jnp.broadcast_to(columns[0:U, n : n + 1], (U, LANES))
    half_weight = weight[...] / STEPS
    sums = jnp.zeros((16, U), F32)
    for n, row in enumerate(
        [half_weight, half_weight * shape[0:1], half_weight * shape[1:2], half_weight * shape[2:3]]
    ):
        sums = jnp.where(which == n, row, sums)
    high, low = split(sums)
    sum4[...] = jnp.concatenate([high, high, low, low], axis=1)
    high, low = split(sphere[...])
    mix4[...] = jnp.concatenate([high, high, low, low], axis=1)
    for axis in range(2):
        to_rank = (iota((U, U), 0).astype(F32) == rank[axis : axis + 1]).astype(BF16)
        pack[axis] = jnp.concatenate([to_rank, to_rank], axis=1)
        from_rank = (
            iota((U, LANES), 1).astype(F32) == columns[0:U, RANK_X + axis : RANK_X + axis + 1]
        ) | (
            (iota((U, LANES), 1) - U).astype(F32) == columns[0:U, RANK_X + axis : RANK_X + axis + 1]
        )
        unpack[axis] = from_rank.astype(BF16)

    lane = iota((16, LANES), 1)

    pltpu.make_async_copy(q, q, q_sem.at[0]).wait()

    def start(x, carry):
        for group in range(4):
            part = pl.ds(16 * group, 16)
            shapes = [coef[SHAPE_0 + n, part, :] for n in range(3)]
            for y in range(Y):
                exponent = RATE * field[x, y : y + 1, :]
                for n in range(3):
                    exponent = exponent + shapes[n] * order[n, x, y : y + 1, :]
                value = jnp.exp2(exponent)
                factor[Y * x + y, part, :] = value
                first[x + 1, y + 1, part, :] = value * q[Y * x + y, part, :]
        return carry

    lax.fori_loop(0, X, start, 0, unroll=True)

    waits = []
    for step in range(STEPS):
        cells = grids[step]
        zeros = jnp.zeros((16, LANES), F32)

        def edges(x, carry):
            out = list(carry)
            for group in range(4):
                part = pl.ds(16 * group, 16)
                for y in range(Y):
                    to = 64 * (group // 2) + 2 * (Y * x + y)
                    turned = pltpu.roll(cells[x + 1, y + 1, part, :], to, 1)
                    chosen = (lane == to) | (lane == lax.rem(to + 127, 128))
                    out[group % 2] = jnp.where(chosen, turned, out[group % 2])
            return tuple(out)

        top, bottom = lax.fori_loop(0, X, edges, (zeros, zeros), unroll=True)
        send_z[step, 0:16, :] = top
        send_z[step, 16:32, :] = bottom

        def face_y(x, carry):
            faces = jnp.concatenate([cells[x + 1, 1], cells[x + 1, Y]], axis=1)
            packed = jnp.dot(
                pack[1], jnp.concatenate(split(faces), axis=0), preferred_element_type=F32
            )
            send_y[step, 0, x] = packed[0:HALF, 0:LANES]
            send_y[step, 1, x] = packed[HALF:U, LANES : 2 * LANES]
            return carry

        lax.fori_loop(0, X, face_y, 0, unroll=True)
        for y in range(Y):
            faces = jnp.concatenate([cells[1, y + 1], cells[X, y + 1]], axis=1)
            packed = jnp.dot(
                pack[0], jnp.concatenate(split(faces), axis=0), preferred_element_type=F32
            )
            send_x[step, 0, y] = packed[0:HALF, 0:LANES]
            send_x[step, 1, y] = packed[HALF:U, LANES : 2 * LANES]

        if step == 0:
            pl.semaphore_wait(barrier, 6)
        copies = []
        for n, (src, dst, axis, way) in enumerate(
            [
                (send_z.at[step], recv_z.at[step, 0], "gz", -1),
                (send_z.at[step], recv_z.at[step, 1], "gz", 1),
                (send_y.at[step, 0], recv_y.at[step, :, 0:HALF, :], "gx", -1),
                (send_y.at[step, 1], recv_y.at[step, :, HALF:U, :], "gx", 1),
                (send_x.at[step, 0], recv_x.at[step, :, 0:HALF, :], "gy", -1),
                (send_x.at[step, 1], recv_x.at[step, :, HALF:U, :], "gy", 1),
            ]
        ):
            copy = pltpu.make_async_remote_copy(
                src_ref=src, dst_ref=dst, send_sem=send_sem.at[step, n], recv_sem=recv_sem.at[step, n],
                device_id=neighbour(axis, way), device_id_type=pl.DeviceIdType.MESH,
            )
            copy.start()
            copies.append(copy)
        for copy in copies:
            copy.wait_recv()
        waits += copies

        def place_y(n, carry):
            received = jnp.concatenate([recv_y[step, 2 * n], recv_y[step, 2 * n + 1]], axis=1)
            chosen = jnp.dot(
                unpack[1], jnp.concatenate(split(received), axis=0), preferred_element_type=F32
            )
            for side in (0, Y + 1):
                cells[2 * n + 1, side] = chosen[:, 0:LANES]
                cells[2 * n + 2, side] = chosen[:, LANES : 2 * LANES]
            return carry

        lax.fori_loop(0, X // 2, place_y, 0, unroll=True)
        for y in range(0, Y, 2):
            received = jnp.concatenate([recv_x[step, y], recv_x[step, y + 1]], axis=1)
            chosen = jnp.dot(
                unpack[0], jnp.concatenate(split(received), axis=0), preferred_element_type=F32
            )
            for side in (0, X + 1):
                cells[side, y + 1] = chosen[:, 0:LANES]
                cells[side, y + 2] = chosen[:, LANES : 2 * LANES]

        ends = z_ends(recv_z.at[step])
        pltpu.make_async_copy(forward[step], forward[step], forward_sem.at[step]).wait()
        if step == 0:
            for x in range(X):
                advance(0, x, first, factor, coef, mix4, ends, forward_0, total, nxt=nxt)
        else:
            ends_out[0:16, :] = ends[0]
            ends_out[16:32, :] = ends[1]
    for copy in waits:
        copy.wait_send()


def body(q_dagger, forward, field_iso, field_order, sphere_step, upwind_sign, direction_size, sphere_weight):
    anywhere = pl.BlockSpec(memory_space=pl.ANY)
    inside = pl.BlockSpec(memory_space=pltpu.VMEM)
    cells = (U, ROWS, 1, LANES)
    outer = [
        ((X + 2, Y + 2, U, LANES), F32), ((ROWS, U, LANES), F32), ((ROWS, U, LANES), F32),
        ((ROWS, U, LANES), F32), ((10, U, LANES), F32), ((U, 4 * U), BF16), ((16, 4 * U), BF16),
        ((HALF, LANES), F32),
    ]
    held = pl.pallas_call(
        kernel,
        out_shape=tuple(pltpu.VMEM(shape, kind) for shape, kind in outer),
        in_specs=[pl.BlockSpec(memory_space=pltpu.HBM)] * 8,
        out_specs=(inside,) * 8,
        scratch_shapes=[
            pltpu.VMEM((ROWS, U, LANES), F32),
            pltpu.VMEM((ROWS, U, LANES), F32),
            pltpu.VMEM((X, Y, LANES), F32),
            pltpu.VMEM((3, X, Y, LANES), F32),
            pltpu.VMEM((U, U), F32),
            pltpu.VMEM((3, U), jnp.int32),
            pltpu.VMEM((3, U), F32),
            pltpu.VMEM((1, U), F32),
            pltpu.VMEM((X + 2, Y + 2, U, LANES), F32),
            pltpu.VMEM((LANES, LANES), F32),
            pltpu.VMEM((2, U, 2 * U), BF16),
            pltpu.VMEM((2, U, 2 * U), BF16),
            pltpu.VMEM((STEPS, 2, Y, HALF, LANES), F32),
            pltpu.VMEM((STEPS, 2, X, HALF, LANES), F32),
            pltpu.VMEM((STEPS, HALF, LANES), F32),
            pltpu.VMEM((STEPS, Y, U, LANES), F32),
            pltpu.VMEM((STEPS, X, U, LANES), F32),
            pltpu.VMEM((STEPS, 2, HALF, LANES), F32),
            pltpu.SemaphoreType.DMA((6,)),
            pltpu.SemaphoreType.DMA((1,)),
            pltpu.SemaphoreType.DMA((STEPS,)),
            pltpu.SemaphoreType.DMA((STEPS, 6)),
            pltpu.SemaphoreType.DMA((STEPS, 6)),
        ],
        compiler_params=pltpu.CompilerParams(
            collective_id=0, has_side_effects=True, vmem_limit_bytes=32 * 1024 * 1024
        ),
        name="propagate",
    )(
        *[pltpu.with_memory_space_constraint(array, pltpu.HBM) for array in (
            q_dagger.reshape(cells), forward.reshape((STEPS,) + cells), field_iso, field_order,
            sphere_step, upwind_sign, direction_size, sphere_weight.reshape(1, U),
        )]
    )
    q, density, order = pl.pallas_call(
        finish,
        out_shape=(
            jax.ShapeDtypeStruct(cells, F32),
            jax.ShapeDtypeStruct(field_iso.shape, F32),
            jax.ShapeDtypeStruct(field_order.shape, F32),
        ),
        in_specs=[inside] * 8,
        out_specs=(pl.BlockSpec(memory_space=pltpu.HBM),) * 3,
        scratch_shapes=[
            pltpu.VMEM((ROWS, U, LANES), F32),
            pltpu.VMEM((4, X, Y, LANES), F32),
            pltpu.SemaphoreType.DMA((ROWS + 2,)),
        ],
        compiler_params=pltpu.CompilerParams(vmem_limit_bytes=32 * 1024 * 1024),
        name="finish",
    )(*held)
    return q.reshape(q_dagger.shape), density, order


def solution(mesh):
    grid = P("gy", "gx", "gz")
    placed = (
        P(None, "gy", "gx", "gz"), P(None, None, "gy", "gx", "gz"), grid,
        P(None, "gy", "gx", "gz"), P(), P(), P(), P(),
    )
    return jax.shard_map(
        body, mesh=mesh, in_specs=placed,
        out_specs=(P(None, "gy", "gx", "gz"), grid, P(None, "gy", "gx", "gz")), check_vma=False,
    )
```

```python
import functools
import math

import jax
import jax.numpy as jnp
from jax import lax
from jax.experimental import pallas as pl
from jax.experimental.pallas import tpu as pltpu
from jax.sharding import PartitionSpec as P

U = 64
HALF = U // 2
LANES = 128
X = 8
Y = 4
ROWS = X * Y
STEPS = 2
RATE = -0.2 / math.log(2.0)
F32 = jnp.float32
BF16 = jnp.bfloat16

UP_X, LOW_X, UP_Y, LOW_Y, SPEED_Z, KEEP, SHAPE_0, SHAPE_1, SHAPE_2, SIGN_Z, RANK_X, RANK_Y = range(12)


def split(values):
    high = values.astype(BF16)
    low = (values - high.astype(F32)).astype(BF16)
    return high, low


def iota(shape, dim):
    return lax.broadcasted_iota(jnp.int32, shape, dim)


def neighbour(axis, step):
    count = lax.axis_size(axis)
    return {axis: lax.rem(lax.axis_index(axis) + count + step, count)}


def stacked4(values):
    pair = jnp.concatenate(split(values), axis=0)
    return jnp.concatenate([pair, pair], axis=0)


def mix_own(x, cells, coef, mix4, mixed):
    lane = iota((16, LANES), 1)
    parts = [([], []) for _ in range(Y)]
    for group in range(4):
        part = pl.ds(16 * group, 16)
        up_x, low_x, up_y, low_y, speed_z, kept = [coef[n, part, :] for n in range(6)]
        up_z = coef[SIGN_Z, part, :] > 0.5
        up_speed = jnp.where(up_z & (lane != 127), speed_z, 0.0)
        low_speed = jnp.where(~up_z & (lane != 0), speed_z, 0.0)
        for y in range(Y):
            here = cells[x, y, part, :]
            moved = (
                kept * here
                + up_speed * pltpu.roll(here, 127, 1)
                + low_speed * pltpu.roll(here, 1, 1)
            )
            if x + 1 < X:
                moved = moved + up_x * cells[x + 1, y, part, :]
            if x > 0:
                moved = moved + low_x * cells[x - 1, y, part, :]
            if y + 1 < Y:
                moved = moved + up_y * cells[x, y + 1, part, :]
            if y > 0:
                moved = moved + low_y * cells[x, y - 1, part, :]
            high, low = split(moved)
            parts[y][0].append(high)
            parts[y][1].append(low)
    for y in range(0, Y, 2):
        stack = [jnp.concatenate(parts[n][0] + parts[n][1], axis=0) for n in (y, y + 1)]
        stack = jnp.concatenate(stack, axis=1)
        out = jnp.dot(
            mix4[...], jnp.concatenate([stack, stack], axis=0), preferred_element_type=F32
        )
        for n in range(2):
            mixed[Y * x + y + n] = out[:, LANES * n : LANES * (n + 1)]


def mix_ends(recv, coef, mix4):
    lane = iota((HALF, LANES), 1)
    ends = jnp.where(lane % 2 == 0, recv[0], pltpu.roll(recv[1], 2, 1))
    ends = jnp.concatenate([ends, pltpu.roll(ends, 64, 1)], axis=0)
    upper = iota((U, LANES), 1) % 2 == 0
    wanted = upper == (coef[SIGN_Z] > 0.5)
    ends = jnp.where(wanted, coef[SPEED_Z] * ends, 0.0)
    return jnp.dot(mix4[...], stacked4(ends), preferred_element_type=F32)


def add_sides(recv, side4, mixed, rows):
    for way in range(2):
        part = pl.ds(HALF * way, HALF)
        for place in range(0, len(rows[way]), 2):
            pair = jnp.concatenate([recv[place, part, :], recv[place + 1, part, :]], axis=1)
            out = jnp.dot(side4[way], stacked4(pair), preferred_element_type=F32)
            for n in range(2):
                row = rows[way][place + n]
                mixed[row] = mixed[row] + out[:, LANES * n : LANES * (n + 1)]


def whole(row, mixed, end_terms):
    lane = iota((U, LANES), 1)
    edge = (lane == 0) | (lane == 127)
    return mixed[row] + jnp.where(edge, pltpu.roll(end_terms, (127 - 2 * row) % 128, 1), 0.0)


def finish(
    mixed, factor, total, forward, sum4, end_terms, out_q, out_density, out_order, q, dens, store_sem
):
    copies = []
    terms = end_terms[...]
    for first in range(0, ROWS, 2):
        sums = []
        for row in (first, first + 1):
            value = factor[row] * whole(row, mixed, terms)
            q[row] = value
            copy = pltpu.make_async_copy(q.at[row], out_q.at[:, row, 0, :], store_sem.at[row])
            copy.start()
            copies.append(copy)
            sums.append(jnp.concatenate(split(total[row] + forward[row] * value), axis=0))
        sums = jnp.concatenate(sums, axis=1)
        summed = jnp.dot(
            sum4[...], jnp.concatenate([sums, sums], axis=0), preferred_element_type=F32
        )
        for n in range(2):
            x, y = divmod(first + n, Y)
            for a in range(4):
                dens[a, x, y : y + 1, :] = summed[a : a + 1, LANES * n : LANES * (n + 1)]
    for copy in (
        pltpu.make_async_copy(dens.at[0], out_density, store_sem.at[ROWS]),
        pltpu.make_async_copy(dens.at[1:4], out_order, store_sem.at[ROWS + 1]),
    ):
        copy.start()
        copies.append(copy)
    for copy in copies:
        copy.wait()


def kernel(
    q_hbm, forward_hbm, iso_hbm, order_hbm, sphere_hbm, sign_hbm, size_hbm, weight_hbm,
    mixed, factor, total, forward_1, sum4, terms_out,
    q, forward_0, field, order, sphere, sign, size, weight,
    cells_0, cells_1, coef, table, mix4, pack, side4,
    send_x, send_y, send_z, recv_x, recv_y, recv_z,
    load_sem, q_sem, forward_sem, send_sem, recv_sem,
):
    forward = (forward_0, forward_1)
    grids = (cells_0, cells_1)
    barrier = pltpu.get_barrier_semaphore()
    for axis in ("gx", "gy", "gz"):
        for way in (1, -1):
            pl.semaphore_signal(
                barrier, inc=1, device_id=neighbour(axis, way), device_id_type=pl.DeviceIdType.MESH
            )

    small = [
        pltpu.make_async_copy(src, dst, load_sem.at[n])
        for n, (src, dst) in enumerate(
            [(sign_hbm, sign), (size_hbm, size), (iso_hbm, field), (order_hbm, order),
             (weight_hbm, weight), (sphere_hbm, sphere)]
        )
    ]
    for copy in small:
        copy.start()

    def load_q(row, carry):
        pltpu.make_async_copy(q_hbm.at[:, row, 0, :], q.at[row], q_sem.at[0]).start()
        return carry

    lax.fori_loop(0, ROWS, load_q, 0)

    small[0].wait()
    small[1].wait()
    signs = sign[...].astype(F32)
    signed = (2.0 * signs - 1.0) * size[...]
    length = jnp.sqrt(jnp.sum(signed * signed, axis=0, keepdims=True))
    along = signed / length
    shape = along * along - 1.0 / 3.0
    speed = 0.5 * jnp.abs(along)
    below = (iota((U, U), 0) < iota((U, U), 1)).astype(BF16)
    ones_before = jnp.dot(signs.astype(BF16), below, preferred_element_type=F32)
    place = iota((1, U), 1).astype(F32)
    rank = jnp.where(signs > 0.5, ones_before, HALF + place - ones_before)
    keep = 1.0 - jnp.sum(speed, axis=0, keepdims=True)
    upper = speed * signs
    lower = speed * (1.0 - signs)
    rows = [
        upper[0:1], lower[0:1], upper[1:2], lower[1:2], speed[2:3], keep,
        RATE * shape[0:1], RATE * shape[1:2], RATE * shape[2:3],
        signs[2:3], rank[0:1], rank[1:2],
    ]
    stacked = jnp.zeros((16, U), F32)
    which = iota((16, U), 0)
    for n, row in enumerate(rows):
        stacked = jnp.where(which == n, row, stacked)
    table[...] = jnp.zeros((LANES, LANES), F32)
    table[0:16, 0:U] = stacked
    columns = jnp.transpose(table[...])
    for n in range(10):
        coef[n] = jnp.broadcast_to(columns[0:U, n : n + 1], (U, LANES))
    for axis in range(2):
        to_rank = (iota((U, U), 0).astype(F32) == rank[axis : axis + 1]).astype(BF16)
        pack[axis] = jnp.concatenate([to_rank, to_rank], axis=1)

    lane = iota((16, LANES), 1)

    small[2].wait()
    small[3].wait()
    pltpu.make_async_copy(q, q, q_sem.at[0]).wait()
    for x in range(X):
        for group in range(4):
            part = pl.ds(16 * group, 16)
            shapes = [coef[SHAPE_0 + n, part, :] for n in range(3)]
            for y in range(Y):
                exponent = RATE * field[x, y : y + 1, :]
                for n in range(3):
                    exponent = exponent + shapes[n] * order[n, x, y : y + 1, :]
                value = jnp.exp2(exponent)
                factor[Y * x + y, part, :] = value
                cells_0[x, y, part, :] = value * q[Y * x + y, part, :]

    waits = []
    for step in range(STEPS):
        cells = grids[step]

        def send(n, src, dst, axis, way):
            copy = pltpu.make_async_remote_copy(
                src_ref=src, dst_ref=dst, send_sem=send_sem.at[step, n], recv_sem=recv_sem.at[step, n],
                device_id=neighbour(axis, way), device_id_type=pl.DeviceIdType.MESH,
            )
            copy.start()
            waits.append(copy)
            return copy

        ends = [jnp.zeros((16, LANES), F32)] * 2
        for x in range(X):
            for group in range(4):
                part = pl.ds(16 * group, 16)
                for y in range(Y):
                    to = 64 * (group // 2) + 2 * (Y * x + y)
                    turned = pltpu.roll(cells[x, y, part, :], to, 1)
                    chosen = (lane == to) | (lane == (to + 127) % 128)
                    ends[group % 2] = jnp.where(chosen, turned, ends[group % 2])
        send_z[step, 0:16, :] = ends[0]
        send_z[step, 16:32, :] = ends[1]
        if step == 0:
            pl.semaphore_wait(barrier, 6)
        come_z = [
            send(0, send_z.at[step], recv_z.at[step, 0], "gz", -1),
            send(1, send_z.at[step], recv_z.at[step, 1], "gz", 1),
        ]
        for x in range(X):
            faces = jnp.concatenate([cells[x, 0], cells[x, Y - 1]], axis=1)
            packed = jnp.dot(
                pack[1], jnp.concatenate(split(faces), axis=0), preferred_element_type=F32
            )
            send_y[step, 0, x] = packed[0:HALF, 0:LANES]
            send_y[step, 1, x] = packed[HALF:U, LANES : 2 * LANES]
        come_y = [
            send(2, send_y.at[step, 0], recv_y.at[step, :, 0:HALF, :], "gx", -1),
            send(3, send_y.at[step, 1], recv_y.at[step, :, HALF:U, :], "gx", 1),
        ]
        for y in range(Y):
            faces = jnp.concatenate([cells[0, y], cells[X - 1, y]], axis=1)
            packed = jnp.dot(
                pack[0], jnp.concatenate(split(faces), axis=0), preferred_element_type=F32
            )
            send_x[step, 0, y] = packed[0:HALF, 0:LANES]
            send_x[step, 1, y] = packed[HALF:U, LANES : 2 * LANES]
        come_x = [
            send(4, send_x.at[step, 0], recv_x.at[step, :, 0:HALF, :], "gy", -1),
            send(5, send_x.at[step, 1], recv_x.at[step, :, HALF:U, :], "gy", 1),
        ]

        if step == 0:
            def load_forward(row, carry):
                for n in range(STEPS):
                    pltpu.make_async_copy(
                        forward_hbm.at[n, :, row, 0, :], forward[n].at[row], forward_sem.at[n]
                    ).start()
                return carry

            lax.fori_loop(0, ROWS, load_forward, 0)
            small[4].wait()
            small[5].wait()
            half_weight = weight[...] / STEPS
            sums = jnp.zeros((16, U), F32)
            for n, row in enumerate(
                [half_weight] + [half_weight * shape[a : a + 1] for a in range(3)]
            ):
                sums = jnp.where(which == n, row, sums)
            high, low = split(sums)
            sum4[...] = jnp.concatenate([high, high, low, low], axis=1)
            high, low = split(sphere[...])
            mix4[...] = jnp.concatenate([high, high, low, low], axis=1)
            for axis in range(2):
                of_rank = columns[0:U, RANK_X + axis : RANK_X + axis + 1]
                from_rank = (iota((U, U), 1).astype(F32) == of_rank).astype(BF16)
                high, low = split(sphere[...] * speed[axis : axis + 1])
                sorted_mix = jnp.dot(
                    jnp.concatenate([high, low], axis=1),
                    jnp.concatenate([from_rank, from_rank], axis=0),
                    preferred_element_type=F32,
                )
                for way in range(2):
                    high, low = split(sorted_mix[:, HALF * way : HALF * (way + 1)])
                    side4[axis, way] = jnp.concatenate([high, high, low, low], axis=1)

        for x in range(X):
            mix_own(x, cells, coef, mix4, mixed)
        if step == 0:
            for n in range(STEPS):
                pltpu.make_async_copy(forward[n], forward[n], forward_sem.at[n]).wait()

        for copy in come_z:
            copy.wait_recv()
        terms = mix_ends(recv_z.at[step], coef, mix4)
        for copy in come_x:
            copy.wait_recv()
        add_sides(
            recv_x.at[step], side4.at[0], mixed,
            [[Y * (X - 1) + y for y in range(Y)], list(range(Y))],
        )
        for copy in come_y:
            copy.wait_recv()
        add_sides(
            recv_y.at[step], side4.at[1], mixed,
            [[Y * x + Y - 1 for x in range(X)], [Y * x for x in range(X)]],
        )
        if step == 0:
            for row in range(ROWS):
                value = factor[row] * whole(row, mixed, terms)
                cells_1[row // Y, row % Y] = factor[row] * value
                total[row] = forward_0[row] * value
        else:
            terms_out[...] = terms
    for copy in waits:
        copy.wait_send()


def body(q_dagger, forward, field_iso, field_order, sphere_step, upwind_sign, direction_size, sphere_weight):
    outside = pl.BlockSpec(memory_space=pltpu.HBM)
    inside = pl.BlockSpec(memory_space=pltpu.VMEM)
    cells = (U, ROWS, 1, LANES)
    block = pltpu.VMEM((ROWS, U, LANES), F32)
    held = pl.pallas_call(
        kernel,
        out_shape=(
            block, block, block, block, pltpu.VMEM((16, 4 * U), BF16), pltpu.VMEM((U, LANES), F32)
        ),
        in_specs=[outside] * 8,
        out_specs=(inside,) * 6,
        scratch_shapes=[
            block,
            block,
            pltpu.VMEM((X, Y, LANES), F32),
            pltpu.VMEM((3, X, Y, LANES), F32),
            pltpu.VMEM((U, U), F32),
            pltpu.VMEM((3, U), jnp.int32),
            pltpu.VMEM((3, U), F32),
            pltpu.VMEM((1, U), F32),
            pltpu.VMEM((X, Y, U, LANES), F32),
            pltpu.VMEM((X, Y, U, LANES), F32),
            pltpu.VMEM((10, U, LANES), F32),
            pltpu.VMEM((LANES, LANES), F32),
            pltpu.VMEM((U, 4 * U), BF16),
            pltpu.VMEM((2, U, 2 * U), BF16),
            pltpu.VMEM((2, 2, U, LANES), BF16),
            pltpu.VMEM((STEPS, 2, Y, HALF, LANES), F32),
            pltpu.VMEM((STEPS, 2, X, HALF, LANES), F32),
            pltpu.VMEM((STEPS, HALF, LANES), F32),
            pltpu.VMEM((STEPS, Y, U, LANES), F32),
            pltpu.VMEM((STEPS, X, U, LANES), F32),
            pltpu.VMEM((STEPS, 2, HALF, LANES), F32),
            pltpu.SemaphoreType.DMA((6,)),
            pltpu.SemaphoreType.DMA((1,)),
            pltpu.SemaphoreType.DMA((STEPS,)),
            pltpu.SemaphoreType.DMA((STEPS, 6)),
            pltpu.SemaphoreType.DMA((STEPS, 6)),
        ],
        compiler_params=pltpu.CompilerParams(
            collective_id=0, has_side_effects=True, vmem_limit_bytes=32 * 1024 * 1024
        ),
        name="propagate",
    )(
        *[pltpu.with_memory_space_constraint(array, pltpu.HBM) for array in (
            q_dagger.reshape(cells), forward.reshape((STEPS,) + cells), field_iso, field_order,
            sphere_step, upwind_sign, direction_size, sphere_weight.reshape(1, U),
        )]
    )
    q, density, order = pl.pallas_call(
        finish,
        out_shape=(
            jax.ShapeDtypeStruct(cells, F32),
            jax.ShapeDtypeStruct(field_iso.shape, F32),
            jax.ShapeDtypeStruct(field_order.shape, F32),
        ),
        in_specs=[inside] * 6,
        out_specs=(outside,) * 3,
        scratch_shapes=[
            block,
            pltpu.VMEM((4, X, Y, LANES), F32),
            pltpu.SemaphoreType.DMA((ROWS + 2,)),
        ],
        compiler_params=pltpu.CompilerParams(vmem_limit_bytes=32 * 1024 * 1024),
        name="finish",
    )(*held)
    return q.reshape(q_dagger.shape), density, order


def solution(mesh):
    grid = P("gy", "gx", "gz")
    placed = (
        P(None, "gy", "gx", "gz"), P(None, None, "gy", "gx", "gz"), grid,
        P(None, "gy", "gx", "gz"), P(), P(), P(), P(),
    )
    return jax.shard_map(
        body, mesh=mesh, in_specs=placed,
        out_specs=(P(None, "gy", "gx", "gz"), grid, P(None, "gy", "gx", "gz")), check_vma=False,
    )
```

```python
import functools
import math

import jax
import jax.numpy as jnp
from jax import lax
from jax.experimental import pallas as pl
from jax.experimental.pallas import tpu as pltpu
from jax.sharding import PartitionSpec as P

U = 64
HALF = U // 2
LANES = 128
X = 8
Y = 4
ROWS = X * Y
STEPS = 2
SIDES = [("gz", -1), ("gz", 1), ("gx", -1), ("gx", 1), ("gy", -1), ("gy", 1)]
RATE = -0.2 / math.log(2.0)
F32 = jnp.float32
BF16 = jnp.bfloat16

UP_X, LOW_X, UP_Y, LOW_Y, SPEED_Z, KEEP, SHAPE_0, SHAPE_1, SHAPE_2, SIGN_Z = range(10)


def split(values):
    high = values.astype(BF16)
    low = (values - high.astype(F32)).astype(BF16)
    return high, low


def iota(shape, dim):
    return lax.broadcasted_iota(jnp.int32, shape, dim)


def stacked4(values):
    pair = jnp.concatenate(split(values), axis=0)
    return jnp.concatenate([pair, pair], axis=0)


def mix_own(x, cells, coef, mix4, mixed):
    lane = iota((16, LANES), 1)
    parts = [([], []) for _ in range(Y)]
    for group in range(4):
        part = pl.ds(16 * group, 16)
        up_x, low_x, up_y, low_y, speed_z, kept = [coef[n, part, :] for n in range(6)]
        up_z = coef[SIGN_Z, part, :] > 0.5
        up_speed = jnp.where(up_z & (lane != 127), speed_z, 0.0)
        low_speed = jnp.where(~up_z & (lane != 0), speed_z, 0.0)
        for y in range(Y):
            here = cells[x, y, part, :]
            moved = (
                kept * here
                + up_speed * pltpu.roll(here, 127, 1)
                + low_speed * pltpu.roll(here, 1, 1)
            )
            if x + 1 < X:
                moved = moved + up_x * cells[x + 1, y, part, :]
            if x > 0:
                moved = moved + low_x * cells[x - 1, y, part, :]
            if y + 1 < Y:
                moved = moved + up_y * cells[x, y + 1, part, :]
            if y > 0:
                moved = moved + low_y * cells[x, y - 1, part, :]
            high, low = split(moved)
            parts[y][0].append(high)
            parts[y][1].append(low)
    for y in range(0, Y, 2):
        stack = [jnp.concatenate(parts[n][0] + parts[n][1], axis=0) for n in (y, y + 1)]
        stack = jnp.concatenate(stack, axis=1)
        out = jnp.dot(
            mix4[...], jnp.concatenate([stack, stack], axis=0), preferred_element_type=F32
        )
        for n in range(2):
            mixed[Y * x + y + n] = out[:, LANES * n : LANES * (n + 1)]


def mix_ends(recv, coef, mix4):
    lane = iota((HALF, LANES), 1)
    ends = jnp.where(lane % 2 == 0, recv[0], pltpu.roll(recv[1], 2, 1))
    ends = jnp.concatenate([ends, pltpu.roll(ends, 64, 1)], axis=0)
    upper = iota((U, LANES), 1) % 2 == 0
    wanted = upper == (coef[SIGN_Z] > 0.5)
    ends = jnp.where(wanted, coef[SPEED_Z] * ends, 0.0)
    return jnp.dot(mix4[...], stacked4(ends), preferred_element_type=F32)


def add_sides(recv, side4, mixed, rows):
    for way in range(2):
        part = pl.ds(HALF * way, HALF)
        for place in range(0, len(rows[way]), 2):
            pair = jnp.concatenate([recv[place, part, :], recv[place + 1, part, :]], axis=1)
            out = jnp.dot(side4[way], stacked4(pair), preferred_element_type=F32)
            for n in range(2):
                row = rows[way][place + n]
                mixed[row] = mixed[row] + out[:, LANES * n : LANES * (n + 1)]


def whole(row, mixed, end_terms):
    lane = iota((U, LANES), 1)
    edge = (lane == 0) | (lane == 127)
    return mixed[row] + jnp.where(edge, pltpu.roll(end_terms, (127 - 2 * row) % 128, 1), 0.0)


def finish(
    mixed, factor, total, forward, sum4, end_terms, out_q, out_density, out_order, q, dens, store_sem
):
    copies = []
    terms = end_terms[...]
    for row in range(ROWS):
        q[row] = factor[row] * whole(row, mixed, terms)
        copy = pltpu.make_async_copy(q.at[row], out_q.at[:, row, 0, :], store_sem.at[row])
        copy.start()
        copies.append(copy)
    for first in range(0, ROWS, 2):
        sums = [
            jnp.concatenate(split(total[row] + forward[row] * q[row]), axis=0)
            for row in (first, first + 1)
        ]
        sums = jnp.concatenate(sums, axis=1)
        summed = jnp.dot(
            sum4[...], jnp.concatenate([sums, sums], axis=0), preferred_element_type=F32
        )
        for n in range(2):
            x, y = divmod(first + n, Y)
            for a in range(4):
                dens[a, x, y : y + 1, :] = summed[a : a + 1, LANES * n : LANES * (n + 1)]
    for copy in (
        pltpu.make_async_copy(dens.at[0], out_density, store_sem.at[ROWS]),
        pltpu.make_async_copy(dens.at[1:4], out_order, store_sem.at[ROWS + 1]),
    ):
        copy.start()
        copies.append(copy)
    for copy in copies:
        copy.wait()


def kernel(
    q_hbm, forward_hbm, iso_hbm, order_hbm, sphere_hbm, sign_hbm, size_hbm, weight_hbm,
    mixed, factor, total, forward_1, sum4, terms_out,
    q, forward_0, field, order, sphere, sign, size, weight,
    cells_0, cells_1, coef, table, mix4, pack, side4,
    send_x, send_y, send_z, recv_x, recv_y, recv_z,
    load_sem, q_sem, forward_sem, send_sem, recv_sem, ready,
):
    forward = (forward_0, forward_1)
    grids = (cells_0, cells_1)
    barrier = pltpu.get_barrier_semaphore()
    here = [lax.axis_index(axis) for axis, _ in SIDES]
    there = [
        lax.rem(index + lax.axis_size(axis) + way, lax.axis_size(axis))
        for index, (axis, way) in zip(here, SIDES)
    ]
    lower = jnp.int32(0)
    for n, (axis, way) in enumerate(SIDES):
        lower = lower + (there[n] < here[n]).astype(jnp.int32)

        @pl.when(there[n] > here[n])
        def _():
            pl.semaphore_signal(
                barrier, inc=1, device_id={axis: there[n]}, device_id_type=pl.DeviceIdType.MESH
            )

    small = [
        pltpu.make_async_copy(src, dst, load_sem.at[n])
        for n, (src, dst) in enumerate(
            [(sign_hbm, sign), (size_hbm, size), (iso_hbm, field), (order_hbm, order),
             (weight_hbm, weight), (sphere_hbm, sphere)]
        )
    ]
    for copy in small:
        copy.start()

    def load_q(row, carry):
        pltpu.make_async_copy(q_hbm.at[:, row, 0, :], q.at[row], q_sem.at[0]).start()
        return carry

    lax.fori_loop(0, ROWS, load_q, 0)

    @pl.when(lower > 0)
    def _():
        pl.semaphore_wait(barrier, lower)

    for n, (axis, way) in enumerate(SIDES):

        @pl.when(there[n] < here[n])
        def _():
            pl.semaphore_signal(
                ready.at[n ^ 1], inc=1, device_id={axis: there[n]}, device_id_type=pl.DeviceIdType.MESH
            )


    small[0].wait()
    small[1].wait()
    signs = sign[...].astype(F32)
    signed = (2.0 * signs - 1.0) * size[...]
    length = jnp.sqrt(jnp.sum(signed * signed, axis=0, keepdims=True))
    along = signed / length
    shape = along * along - 1.0 / 3.0
    speed = 0.5 * jnp.abs(along)
    keep = 1.0 - jnp.sum(speed, axis=0, keepdims=True)
    upper = speed * signs
    lower = speed * (1.0 - signs)
    rows = [
        upper[0:1], lower[0:1], upper[1:2], lower[1:2], speed[2:3], keep,
        RATE * shape[0:1], RATE * shape[1:2], RATE * shape[2:3], signs[2:3],
    ]
    which = iota((16, U), 0)

    def turned(rows):
        stacked = jnp.zeros((16, U), F32)
        for n, row in enumerate(rows):
            stacked = jnp.where(which == n, row, stacked)
        table[:, 0:U] = stacked
        return jnp.transpose(table[...])

    table[...] = jnp.zeros((16, LANES), F32)
    columns = turned(rows)
    for n in (SHAPE_0, SHAPE_1, SHAPE_2):
        coef[n] = jnp.broadcast_to(columns[0:U, n : n + 1], (U, LANES))
    below = (iota((U, U), 0) < iota((U, U), 1)).astype(BF16)
    ones_before = jnp.dot(signs.astype(BF16), below, preferred_element_type=F32)
    place = iota((1, U), 1).astype(F32)
    rank = jnp.where(signs > 0.5, ones_before, HALF + place - ones_before)
    for axis in range(2):
        to_rank = (iota((U, U), 0).astype(F32) == rank[axis : axis + 1]).astype(BF16)
        pack[axis] = jnp.concatenate([to_rank, to_rank], axis=1)

    lane = iota((16, LANES), 1)

    small[2].wait()
    small[3].wait()
    pltpu.make_async_copy(q, q, q_sem.at[0]).wait()
    for x in range(X):
        for group in range(4):
            part = pl.ds(16 * group, 16)
            shapes = [coef[SHAPE_0 + n, part, :] for n in range(3)]
            for y in range(Y):
                exponent = RATE * field[x, y : y + 1, :]
                for n in range(3):
                    exponent = exponent + shapes[n] * order[n, x, y : y + 1, :]
                value = jnp.exp2(exponent)
                factor[Y * x + y, part, :] = value
                cells_0[x, y, part, :] = value * q[Y * x + y, part, :]

    waits = []
    for step in range(STEPS):
        cells = grids[step]

        def send(n, src, dst):
            axis, way = SIDES[n]
            copy = pltpu.make_async_remote_copy(
                src_ref=src, dst_ref=dst, send_sem=send_sem.at[step, n], recv_sem=recv_sem.at[step, n],
                device_id={axis: there[n]}, device_id_type=pl.DeviceIdType.MESH,
            )
            if step > 0:
                copy.start()
            waits.append(copy)
            return copy

        ends = [jnp.zeros((16, LANES), F32)] * 2
        for x in range(X):
            for group in range(4):
                part = pl.ds(16 * group, 16)
                for y in range(Y):
                    to = 64 * (group // 2) + 2 * (Y * x + y)
                    rolled = pltpu.roll(cells[x, y, part, :], to, 1)
                    chosen = (lane == to) | (lane == (to + 127) % 128)
                    ends[group % 2] = jnp.where(chosen, rolled, ends[group % 2])
        send_z[step, 0:16, :] = ends[0]
        send_z[step, 16:32, :] = ends[1]
        come_z = [
            send(0, send_z.at[step], recv_z.at[step, 0]),
            send(1, send_z.at[step], recv_z.at[step, 1]),
        ]
        for x in range(X):
            faces = jnp.concatenate([cells[x, 0], cells[x, Y - 1]], axis=1)
            packed = jnp.dot(
                pack[1], jnp.concatenate(split(faces), axis=0), preferred_element_type=F32
            )
            send_y[step, 0, x] = packed[0:HALF, 0:LANES]
            send_y[step, 1, x] = packed[HALF:U, LANES : 2 * LANES]
        come_y = [
            send(2, send_y.at[step, 0], recv_y.at[step, :, 0:HALF, :]),
            send(3, send_y.at[step, 1], recv_y.at[step, :, HALF:U, :]),
        ]
        for y in range(Y):
            faces = jnp.concatenate([cells[0, y], cells[X - 1, y]], axis=1)
            packed = jnp.dot(
                pack[0], jnp.concatenate(split(faces), axis=0), preferred_element_type=F32
            )
            send_x[step, 0, y] = packed[0:HALF, 0:LANES]
            send_x[step, 1, y] = packed[HALF:U, LANES : 2 * LANES]
        come_x = [
            send(4, send_x.at[step, 0], recv_x.at[step, :, 0:HALF, :]),
            send(5, send_x.at[step, 1], recv_x.at[step, :, HALF:U, :]),
        ]

        if step == 0:
            far = [
                (there[n] > here[n] + 1) | ((there[n] == 2) if axis == "gz" else False)
                for n, (axis, way) in enumerate(SIDES)
            ]
            for n in range(6):
                pl.when(there[n] < here[n])(waits[n].start)

            def meet(n):
                pl.semaphore_wait(ready.at[n], 1)
                waits[n].start()

            for n in (1, 5, 3, 0, 4, 2):
                pl.when((there[n] > here[n]) & ~far[n])(functools.partial(meet, n))
            for n in (1, 0, 5, 4, 3, 2):
                pl.when((there[n] > here[n]) & far[n])(functools.partial(meet, n))

        if step == 0:
            for n in range(10):
                if n not in (SHAPE_0, SHAPE_1, SHAPE_2):
                    coef[n] = jnp.broadcast_to(columns[0:U, n : n + 1], (U, LANES))
            ranks = turned([rank[0:1], rank[1:2]])

            def load_forward(row, carry):
                for n in range(STEPS):
                    pltpu.make_async_copy(
                        forward_hbm.at[n, :, row, 0, :], forward[n].at[row], forward_sem.at[n]
                    ).start()
                return carry

            lax.fori_loop(0, ROWS, load_forward, 0)
            small[4].wait()
            small[5].wait()
            half_weight = weight[...] / STEPS
            sums = jnp.zeros((16, U), F32)
            for n, row in enumerate(
                [half_weight] + [half_weight * shape[a : a + 1] for a in range(3)]
            ):
                sums = jnp.where(which == n, row, sums)
            high, low = split(sums)
            sum4[...] = jnp.concatenate([high, high, low, low], axis=1)
            high, low = split(sphere[...])
            mix4[...] = jnp.concatenate([high, high, low, low], axis=1)
            for axis in range(2):
                of_rank = ranks[0:U, axis : axis + 1]
                from_rank = (iota((U, U), 1).astype(F32) == of_rank).astype(BF16)
                high, low = split(sphere[...] * speed[axis : axis + 1])
                sorted_mix = jnp.dot(
                    jnp.concatenate([high, low], axis=1),
                    jnp.concatenate([from_rank, from_rank], axis=0),
                    preferred_element_type=F32,
                )
                for way in range(2):
                    high, low = split(sorted_mix[:, HALF * way : HALF * (way + 1)])
                    side4[axis, way] = jnp.concatenate([high, high, low, low], axis=1)

        for x in range(X):
            mix_own(x, cells, coef, mix4, mixed)
        if step == 0:
            for n in range(STEPS):
                pltpu.make_async_copy(forward[n], forward[n], forward_sem.at[n]).wait()

        for copy in come_z:
            copy.wait_recv()
        terms = mix_ends(recv_z.at[step], coef, mix4)
        for copy in come_x:
            copy.wait_recv()
        add_sides(
            recv_x.at[step], side4.at[0], mixed,
            [[Y * (X - 1) + y for y in range(Y)], list(range(Y))],
        )
        for copy in come_y:
            copy.wait_recv()
        add_sides(
            recv_y.at[step], side4.at[1], mixed,
            [[Y * x + Y - 1 for x in range(X)], [Y * x for x in range(X)]],
        )
        if step == 0:
            for row in range(ROWS):
                value = factor[row] * whole(row, mixed, terms)
                cells_1[row // Y, row % Y] = factor[row] * value
                total[row] = forward_0[row] * value
        else:
            terms_out[...] = terms
    for copy in waits:
        copy.wait_send()


def body(q_dagger, forward, field_iso, field_order, sphere_step, upwind_sign, direction_size, sphere_weight):
    outside = pl.BlockSpec(memory_space=pltpu.HBM)
    inside = pl.BlockSpec(memory_space=pltpu.VMEM)
    cells = (U, ROWS, 1, LANES)
    block = pltpu.VMEM((ROWS, U, LANES), F32)
    held = pl.pallas_call(
        kernel,
        out_shape=(
            block, block, block, block, pltpu.VMEM((16, 4 * U), BF16), pltpu.VMEM((U, LANES), F32)
        ),
        in_specs=[outside] * 8,
        out_specs=(inside,) * 6,
        scratch_shapes=[
            block,
            block,
            pltpu.VMEM((X, Y, LANES), F32),
            pltpu.VMEM((3, X, Y, LANES), F32),
            pltpu.VMEM((U, U), F32),
            pltpu.VMEM((3, U), jnp.int32),
            pltpu.VMEM((3, U), F32),
            pltpu.VMEM((1, U), F32),
            pltpu.VMEM((X, Y, U, LANES), F32),
            pltpu.VMEM((X, Y, U, LANES), F32),
            pltpu.VMEM((10, U, LANES), F32),
            pltpu.VMEM((16, LANES), F32),
            pltpu.VMEM((U, 4 * U), BF16),
            pltpu.VMEM((2, U, 2 * U), BF16),
            pltpu.VMEM((2, 2, U, LANES), BF16),
            pltpu.VMEM((STEPS, 2, Y, HALF, LANES), F32),
            pltpu.VMEM((STEPS, 2, X, HALF, LANES), F32),
            pltpu.VMEM((STEPS, HALF, LANES), F32),
            pltpu.VMEM((STEPS, Y, U, LANES), F32),
            pltpu.VMEM((STEPS, X, U, LANES), F32),
            pltpu.VMEM((STEPS, 2, HALF, LANES), F32),
            pltpu.SemaphoreType.DMA((6,)),
            pltpu.SemaphoreType.DMA((1,)),
            pltpu.SemaphoreType.DMA((STEPS,)),
            pltpu.SemaphoreType.DMA((STEPS, 6)),
            pltpu.SemaphoreType.DMA((STEPS, 6)),
            pltpu.SemaphoreType.REGULAR((6,)),
        ],
        compiler_params=pltpu.CompilerParams(
            collective_id=0, has_side_effects=True, vmem_limit_bytes=32 * 1024 * 1024
        ),
        name="propagate",
    )(
        *[pltpu.with_memory_space_constraint(array, pltpu.HBM) for array in (
            q_dagger.reshape(cells), forward.reshape((STEPS,) + cells), field_iso, field_order,
            sphere_step, upwind_sign, direction_size, sphere_weight.reshape(1, U),
        )]
    )
    q, density, order = pl.pallas_call(
        finish,
        out_shape=(
            jax.ShapeDtypeStruct(cells, F32),
            jax.ShapeDtypeStruct(field_iso.shape, F32),
            jax.ShapeDtypeStruct(field_order.shape, F32),
        ),
        in_specs=[inside] * 6,
        out_specs=(outside,) * 3,
        scratch_shapes=[
            block,
            pltpu.VMEM((4, X, Y, LANES), F32),
            pltpu.SemaphoreType.DMA((ROWS + 2,)),
        ],
        compiler_params=pltpu.CompilerParams(vmem_limit_bytes=32 * 1024 * 1024),
        name="finish",
    )(*held)
    return q.reshape(q_dagger.shape), density, order


def solution(mesh):
    grid = P("gy", "gx", "gz")
    placed = (
        P(None, "gy", "gx", "gz"), P(None, None, "gy", "gx", "gz"), grid,
        P(None, "gy", "gx", "gz"), P(), P(), P(), P(),
    )
    return jax.shard_map(
        body, mesh=mesh, in_specs=placed,
        out_specs=(P(None, "gy", "gx", "gz"), grid, P(None, "gy", "gx", "gz")), check_vma=False,
    )
```

```python
import functools
import math

import jax
import jax.numpy as jnp
from jax import lax
from jax.experimental import pallas as pl
from jax.experimental.pallas import tpu as pltpu
from jax.sharding import PartitionSpec as P

U = 64
HALF = U // 2
LANES = 128
X = 8
Y = 4
ROWS = X * Y
STEPS = 2
SIDES = [("gz", -1), ("gz", 1), ("gx", -1), ("gx", 1), ("gy", -1), ("gy", 1)]
RATE = -0.2 / math.log(2.0)
F32 = jnp.float32
BF16 = jnp.bfloat16

UP_X, LOW_X, UP_Y, LOW_Y, SPEED_Z, KEEP, SHAPE_0, SHAPE_1, SHAPE_2, SIGN_Z = range(10)


def split(values):
    high = values.astype(BF16)
    low = (values - high.astype(F32)).astype(BF16)
    return high, low


def iota(shape, dim):
    return lax.broadcasted_iota(jnp.int32, shape, dim)


def stacked4(values):
    pair = jnp.concatenate(split(values), axis=0)
    return jnp.concatenate([pair, pair], axis=0)


def mix_own(x, cells, coef, mix4, mixed):
    lane = iota((16, LANES), 1)
    parts = [([], []) for _ in range(Y)]
    for group in range(4):
        part = pl.ds(16 * group, 16)
        up_x, low_x, up_y, low_y, speed_z, kept = [coef[n, part, :] for n in range(6)]
        up_z = coef[SIGN_Z, part, :] > 0.5
        up_speed = jnp.where(up_z & (lane != 127), speed_z, 0.0)
        low_speed = jnp.where(~up_z & (lane != 0), speed_z, 0.0)
        for y in range(Y):
            here = cells[x, y, part, :]
            moved = (
                kept * here
                + up_speed * pltpu.roll(here, 127, 1)
                + low_speed * pltpu.roll(here, 1, 1)
            )
            if x + 1 < X:
                moved = moved + up_x * cells[x + 1, y, part, :]
            if x > 0:
                moved = moved + low_x * cells[x - 1, y, part, :]
            if y + 1 < Y:
                moved = moved + up_y * cells[x, y + 1, part, :]
            if y > 0:
                moved = moved + low_y * cells[x, y - 1, part, :]
            high, low = split(moved)
            parts[y][0].append(high)
            parts[y][1].append(low)
    for y in range(0, Y, 2):
        stack = [jnp.concatenate(parts[n][0] + parts[n][1], axis=0) for n in (y, y + 1)]
        stack = jnp.concatenate(stack, axis=1)
        out = jnp.dot(
            mix4[...], jnp.concatenate([stack, stack], axis=0), preferred_element_type=F32
        )
        for n in range(2):
            mixed[Y * x + y + n] = out[:, LANES * n : LANES * (n + 1)]


def mix_ends(recv, coef, mix4):
    lane = iota((HALF, LANES), 1)
    ends = jnp.where(lane % 2 == 0, recv[0], pltpu.roll(recv[1], 2, 1))
    ends = jnp.concatenate([ends, pltpu.roll(ends, 64, 1)], axis=0)
    upper = iota((U, LANES), 1) % 2 == 0
    wanted = upper == (coef[SIGN_Z] > 0.5)
    ends = jnp.where(wanted, coef[SPEED_Z] * ends, 0.0)
    return jnp.dot(mix4[...], stacked4(ends), preferred_element_type=F32)


def add_sides(recv, side4, mixed, rows):
    for way in range(2):
        part = pl.ds(HALF * way, HALF)
        for place in range(0, len(rows[way]), 2):
            pair = jnp.concatenate([recv[place, part, :], recv[place + 1, part, :]], axis=1)
            out = jnp.dot(side4[way], stacked4(pair), preferred_element_type=F32)
            for n in range(2):
                row = rows[way][place + n]
                mixed[row] = mixed[row] + out[:, LANES * n : LANES * (n + 1)]


def whole(row, mixed, end_terms):
    lane = iota((U, LANES), 1)
    edge = (lane == 0) | (lane == 127)
    return mixed[row] + jnp.where(edge, pltpu.roll(end_terms, (127 - 2 * row) % 128, 1), 0.0)


def finish(
    mixed, factor, total, forward, sum4, end_terms, out_q, out_density, out_order, q, dens, store_sem
):
    copies = []
    terms = end_terms[...]
    for row in range(ROWS):
        q[row] = factor[row] * whole(row, mixed, terms)
        copy = pltpu.make_async_copy(q.at[row], out_q.at[:, row, 0, :], store_sem.at[row])
        copy.start()
        copies.append(copy)
    for first in range(0, ROWS, 2):
        sums = [
            jnp.concatenate(split(total[row] + forward[row] * q[row]), axis=0)
            for row in (first, first + 1)
        ]
        sums = jnp.concatenate(sums, axis=1)
        summed = jnp.dot(
            sum4[...], jnp.concatenate([sums, sums], axis=0), preferred_element_type=F32
        )
        for n in range(2):
            x, y = divmod(first + n, Y)
            for a in range(4):
                dens[a, x, y : y + 1, :] = summed[a : a + 1, LANES * n : LANES * (n + 1)]
    for copy in (
        pltpu.make_async_copy(dens.at[0], out_density, store_sem.at[ROWS]),
        pltpu.make_async_copy(dens.at[1:4], out_order, store_sem.at[ROWS + 1]),
    ):
        copy.start()
        copies.append(copy)
    for copy in copies:
        copy.wait()


def kernel(
    q_hbm, forward_hbm, iso_hbm, order_hbm, sphere_hbm, sign_hbm, size_hbm, weight_hbm,
    mixed, factor, total, forward_1, sum4, terms_out,
    q, forward_0, field, order, sphere, sign, size, weight,
    cells_0, cells_1, coef, table, mix4, pack, side4,
    send_x, send_y, send_z, recv_x, recv_y, recv_z,
    load_sem, q_sem, forward_sem, send_sem, recv_sem, ready,
):
    forward = (forward_0, forward_1)
    grids = (cells_0, cells_1)
    barrier = pltpu.get_barrier_semaphore()
    here = [lax.axis_index(axis) for axis, _ in SIDES]
    there = [
        lax.rem(index + lax.axis_size(axis) + way, lax.axis_size(axis))
        for index, (axis, way) in zip(here, SIDES)
    ]
    lower = jnp.int32(0)
    for n, (axis, way) in enumerate(SIDES):
        lower = lower + (there[n] < here[n]).astype(jnp.int32)

        @pl.when(there[n] > here[n])
        def _():
            pl.semaphore_signal(
                barrier, inc=1, device_id={axis: there[n]}, device_id_type=pl.DeviceIdType.MESH
            )

    small = [
        pltpu.make_async_copy(src, dst, load_sem.at[n])
        for n, (src, dst) in enumerate(
            [(sign_hbm, sign), (size_hbm, size), (iso_hbm, field), (order_hbm, order),
             (weight_hbm, weight), (sphere_hbm, sphere)]
        )
    ]
    for copy in small:
        copy.start()

    def load_q(row, carry):
        pltpu.make_async_copy(q_hbm.at[:, row, 0, :], q.at[row], q_sem.at[0]).start()
        return carry

    lax.fori_loop(0, ROWS, load_q, 0)

    @pl.when(lower > 0)
    def _():
        pl.semaphore_wait(barrier, lower)

    for n, (axis, way) in enumerate(SIDES):

        @pl.when(there[n] < here[n])
        def _():
            pl.semaphore_signal(
                ready.at[n ^ 1], inc=1, device_id={axis: there[n]}, device_id_type=pl.DeviceIdType.MESH
            )


    small[0].wait()
    small[1].wait()
    signs = sign[...].astype(F32)
    signed = (2.0 * signs - 1.0) * size[...]
    length = jnp.sqrt(jnp.sum(signed * signed, axis=0, keepdims=True))
    along = signed / length
    shape = along * along - 1.0 / 3.0
    speed = 0.5 * jnp.abs(along)
    keep = 1.0 - jnp.sum(speed, axis=0, keepdims=True)
    upper = speed * signs
    lower = speed * (1.0 - signs)
    rows = [
        upper[0:1], lower[0:1], upper[1:2], lower[1:2], speed[2:3], keep,
        RATE * shape[0:1], RATE * shape[1:2], RATE * shape[2:3], signs[2:3],
    ]
    which = iota((16, U), 0)

    def turned(rows):
        stacked = jnp.zeros((16, U), F32)
        for n, row in enumerate(rows):
            stacked = jnp.where(which == n, row, stacked)
        table[:, 0:U] = stacked
        return jnp.transpose(table[...])

    table[...] = jnp.zeros((16, LANES), F32)
    columns = turned(rows)
    for n in (SHAPE_0, SHAPE_1, SHAPE_2):
        coef[n] = jnp.broadcast_to(columns[0:U, n : n + 1], (U, LANES))
    below = (iota((U, U), 0) < iota((U, U), 1)).astype(BF16)
    ones_before = jnp.dot(signs.astype(BF16), below, preferred_element_type=F32)
    place = iota((1, U), 1).astype(F32)
    rank = jnp.where(signs > 0.5, ones_before, HALF + place - ones_before)
    for axis in range(2):
        to_rank = (iota((U, U), 0).astype(F32) == rank[axis : axis + 1]).astype(BF16)
        pack[axis] = jnp.concatenate([to_rank, to_rank], axis=1)

    lane = iota((16, LANES), 1)

    small[2].wait()
    small[3].wait()
    pltpu.make_async_copy(q, q, q_sem.at[0]).wait()
    for x in range(X):
        for group in range(4):
            part = pl.ds(16 * group, 16)
            shapes = [coef[SHAPE_0 + n, part, :] for n in range(3)]
            for y in range(Y):
                exponent = RATE * field[x, y : y + 1, :]
                for n in range(3):
                    exponent = exponent + shapes[n] * order[n, x, y : y + 1, :]
                value = jnp.exp2(exponent)
                factor[Y * x + y, part, :] = value
                cells_0[x, y, part, :] = value * q[Y * x + y, part, :]

    waits = {}
    for step in range(STEPS):
        cells = grids[step]

        def send(n, src, dst):
            axis, way = SIDES[n]
            copy = pltpu.make_async_remote_copy(
                src_ref=src, dst_ref=dst, send_sem=send_sem.at[step, n], recv_sem=recv_sem.at[step, n],
                device_id={axis: there[n]}, device_id_type=pl.DeviceIdType.MESH,
            )
            if step > 0:
                copy.start()
            waits[step, n] = copy
            return copy

        for x in range(X):
            faces = jnp.concatenate([cells[x, 0], cells[x, Y - 1]], axis=1)
            packed = jnp.dot(
                pack[1], jnp.concatenate(split(faces), axis=0), preferred_element_type=F32
            )
            send_y[step, 0, x] = packed[0:HALF, 0:LANES]
            send_y[step, 1, x] = packed[HALF:U, LANES : 2 * LANES]
        come_y = [
            send(2, send_y.at[step, 0], recv_y.at[step, :, 0:HALF, :]),
            send(3, send_y.at[step, 1], recv_y.at[step, :, HALF:U, :]),
        ]
        ends = [jnp.zeros((16, LANES), F32)] * 2
        for x in range(X):
            for group in range(4):
                part = pl.ds(16 * group, 16)
                for y in range(Y):
                    to = 64 * (group // 2) + 2 * (Y * x + y)
                    rolled = pltpu.roll(cells[x, y, part, :], to, 1)
                    chosen = (lane == to) | (lane == (to + 127) % 128)
                    ends[group % 2] = jnp.where(chosen, rolled, ends[group % 2])
        send_z[step, 0:16, :] = ends[0]
        send_z[step, 16:32, :] = ends[1]
        come_z = [
            send(0, send_z.at[step], recv_z.at[step, 0]),
            send(1, send_z.at[step], recv_z.at[step, 1]),
        ]
        for y in range(Y):
            faces = jnp.concatenate([cells[0, y], cells[X - 1, y]], axis=1)
            packed = jnp.dot(
                pack[0], jnp.concatenate(split(faces), axis=0), preferred_element_type=F32
            )
            send_x[step, 0, y] = packed[0:HALF, 0:LANES]
            send_x[step, 1, y] = packed[HALF:U, LANES : 2 * LANES]
        come_x = [
            send(4, send_x.at[step, 0], recv_x.at[step, :, 0:HALF, :]),
            send(5, send_x.at[step, 1], recv_x.at[step, :, HALF:U, :]),
        ]

        if step == 0:
            far = [
                (there[n] > here[n] + 1) | ((there[n] == 2) if axis == "gz" else False)
                for n, (axis, way) in enumerate(SIDES)
            ]
            for n in range(6):
                pl.when(there[n] < here[n])(waits[0, n].start)

            def meet(n):
                pl.semaphore_wait(ready.at[n], 1)
                waits[0, n].start()

            for n in (1, 5, 3, 0, 4, 2):
                pl.when((there[n] > here[n]) & ~far[n])(functools.partial(meet, n))
            for n in (1, 0, 5, 4, 3, 2):
                pl.when((there[n] > here[n]) & far[n])(functools.partial(meet, n))

        if step == 0:
            for n in range(10):
                if n not in (SHAPE_0, SHAPE_1, SHAPE_2):
                    coef[n] = jnp.broadcast_to(columns[0:U, n : n + 1], (U, LANES))
            ranks = turned([rank[0:1], rank[1:2]])

            def load_forward(row, carry):
                for n in range(STEPS):
                    pltpu.make_async_copy(
                        forward_hbm.at[n, :, row, 0, :], forward[n].at[row], forward_sem.at[n]
                    ).start()
                return carry

            lax.fori_loop(0, ROWS, load_forward, 0)
            small[4].wait()
            small[5].wait()
            half_weight = weight[...] / STEPS
            sums = jnp.zeros((16, U), F32)
            for n, row in enumerate(
                [half_weight] + [half_weight * shape[a : a + 1] for a in range(3)]
            ):
                sums = jnp.where(which == n, row, sums)
            high, low = split(sums)
            sum4[...] = jnp.concatenate([high, high, low, low], axis=1)
            high, low = split(sphere[...])
            mix4[...] = jnp.concatenate([high, high, low, low], axis=1)
            for axis in range(2):
                of_rank = ranks[0:U, axis : axis + 1]
                from_rank = (iota((U, U), 1).astype(F32) == of_rank).astype(BF16)
                high, low = split(sphere[...] * speed[axis : axis + 1])
                sorted_mix = jnp.dot(
                    jnp.concatenate([high, low], axis=1),
                    jnp.concatenate([from_rank, from_rank], axis=0),
                    preferred_element_type=F32,
                )
                for way in range(2):
                    high, low = split(sorted_mix[:, HALF * way : HALF * (way + 1)])
                    side4[axis, way] = jnp.concatenate([high, high, low, low], axis=1)

        for x in range(X):
            mix_own(x, cells, coef, mix4, mixed)
        if step == 0:
            for n in range(STEPS):
                pltpu.make_async_copy(forward[n], forward[n], forward_sem.at[n]).wait()

        for copy in come_z:
            copy.wait_recv()
        terms = mix_ends(recv_z.at[step], coef, mix4)
        for copy in come_x:
            copy.wait_recv()
        add_sides(
            recv_x.at[step], side4.at[0], mixed,
            [[Y * (X - 1) + y for y in range(Y)], list(range(Y))],
        )
        def close(ys):
            for row in range(ROWS):
                if row % Y in ys:
                    value = factor[row] * whole(row, mixed, terms)
                    cells_1[row // Y, row % Y] = factor[row] * value
                    total[row] = forward_0[row] * value

        if step == 0:
            close((1, 2))
        for copy in come_y:
            copy.wait_recv()
        add_sides(
            recv_y.at[step], side4.at[1], mixed,
            [[Y * x + Y - 1 for x in range(X)], [Y * x for x in range(X)]],
        )
        if step == 0:
            close((0, Y - 1))
        else:
            terms_out[...] = terms
    for copy in waits.values():
        copy.wait_send()


def body(q_dagger, forward, field_iso, field_order, sphere_step, upwind_sign, direction_size, sphere_weight):
    outside = pl.BlockSpec(memory_space=pltpu.HBM)
    inside = pl.BlockSpec(memory_space=pltpu.VMEM)
    cells = (U, ROWS, 1, LANES)
    block = pltpu.VMEM((ROWS, U, LANES), F32)
    held = pl.pallas_call(
        kernel,
        out_shape=(
            block, block, block, block, pltpu.VMEM((16, 4 * U), BF16), pltpu.VMEM((U, LANES), F32)
        ),
        in_specs=[outside] * 8,
        out_specs=(inside,) * 6,
        scratch_shapes=[
            block,
            block,
            pltpu.VMEM((X, Y, LANES), F32),
            pltpu.VMEM((3, X, Y, LANES), F32),
            pltpu.VMEM((U, U), F32),
            pltpu.VMEM((3, U), jnp.int32),
            pltpu.VMEM((3, U), F32),
            pltpu.VMEM((1, U), F32),
            pltpu.VMEM((X, Y, U, LANES), F32),
            pltpu.VMEM((X, Y, U, LANES), F32),
            pltpu.VMEM((10, U, LANES), F32),
            pltpu.VMEM((16, LANES), F32),
            pltpu.VMEM((U, 4 * U), BF16),
            pltpu.VMEM((2, U, 2 * U), BF16),
            pltpu.VMEM((2, 2, U, LANES), BF16),
            pltpu.VMEM((STEPS, 2, Y, HALF, LANES), F32),
            pltpu.VMEM((STEPS, 2, X, HALF, LANES), F32),
            pltpu.VMEM((STEPS, HALF, LANES), F32),
            pltpu.VMEM((STEPS, Y, U, LANES), F32),
            pltpu.VMEM((STEPS, X, U, LANES), F32),
            pltpu.VMEM((STEPS, 2, HALF, LANES), F32),
            pltpu.SemaphoreType.DMA((6,)),
            pltpu.SemaphoreType.DMA((1,)),
            pltpu.SemaphoreType.DMA((STEPS,)),
            pltpu.SemaphoreType.DMA((STEPS, 6)),
            pltpu.SemaphoreType.DMA((STEPS, 6)),
            pltpu.SemaphoreType.REGULAR((6,)),
        ],
        compiler_params=pltpu.CompilerParams(
            collective_id=0, has_side_effects=True, vmem_limit_bytes=32 * 1024 * 1024
        ),
        name="propagate",
    )(
        *[pltpu.with_memory_space_constraint(array, pltpu.HBM) for array in (
            q_dagger.reshape(cells), forward.reshape((STEPS,) + cells), field_iso, field_order,
            sphere_step, upwind_sign, direction_size, sphere_weight.reshape(1, U),
        )]
    )
    q, density, order = pl.pallas_call(
        finish,
        out_shape=(
            jax.ShapeDtypeStruct(cells, F32),
            jax.ShapeDtypeStruct(field_iso.shape, F32),
            jax.ShapeDtypeStruct(field_order.shape, F32),
        ),
        in_specs=[inside] * 6,
        out_specs=(outside,) * 3,
        scratch_shapes=[
            block,
            pltpu.VMEM((4, X, Y, LANES), F32),
            pltpu.SemaphoreType.DMA((ROWS + 2,)),
        ],
        compiler_params=pltpu.CompilerParams(vmem_limit_bytes=32 * 1024 * 1024),
        name="finish",
    )(*held)
    return q.reshape(q_dagger.shape), density, order


def solution(mesh):
    grid = P("gy", "gx", "gz")
    placed = (
        P(None, "gy", "gx", "gz"), P(None, None, "gy", "gx", "gz"), grid,
        P(None, "gy", "gx", "gz"), P(), P(), P(), P(),
    )
    return jax.shard_map(
        body, mesh=mesh, in_specs=placed,
        out_specs=(P(None, "gy", "gx", "gz"), grid, P(None, "gy", "gx", "gz")), check_vma=False,
    )
```

```python
import functools
import math

import jax
import jax.numpy as jnp
from jax import lax
from jax.experimental import pallas as pl
from jax.experimental.pallas import tpu as pltpu
from jax.sharding import PartitionSpec as P

U = 64
HALF = U // 2
LANES = 128
X = 8
Y = 4
ROWS = X * Y
STEPS = 2
SIDES = [("gz", -1), ("gz", 1), ("gx", -1), ("gx", 1), ("gy", -1), ("gy", 1)]
RATE = -0.2 / math.log(2.0)
F32 = jnp.float32
BF16 = jnp.bfloat16

UP_X, LOW_X, UP_Y, LOW_Y, SPEED_Z, KEEP, SHAPE_0, SHAPE_1, SHAPE_2, SIGN_Z = range(10)


def split(values):
    high = values.astype(BF16)
    low = (values - high.astype(F32)).astype(BF16)
    return high, low


def iota(shape, dim):
    return lax.broadcasted_iota(jnp.int32, shape, dim)


def stacked4(values):
    pair = jnp.concatenate(split(values), axis=0)
    return jnp.concatenate([pair, pair], axis=0)


def mix_own(x, cells, coef, mix4, mixed):
    lane = iota((16, LANES), 1)
    parts = [([], []) for _ in range(Y)]
    for group in range(4):
        part = pl.ds(16 * group, 16)
        up_x, low_x, up_y, low_y, speed_z, kept = [coef[n, part, :] for n in range(6)]
        up_z = coef[SIGN_Z, part, :] > 0.5
        up_speed = jnp.where(up_z & (lane != 127), speed_z, 0.0)
        low_speed = jnp.where(~up_z & (lane != 0), speed_z, 0.0)
        for y in range(Y):
            here = cells[x, y, part, :]
            moved = (
                kept * here
                + up_speed * pltpu.roll(here, 127, 1)
                + low_speed * pltpu.roll(here, 1, 1)
            )
            if x + 1 < X:
                moved = moved + up_x * cells[x + 1, y, part, :]
            if x > 0:
                moved = moved + low_x * cells[x - 1, y, part, :]
            if y + 1 < Y:
                moved = moved + up_y * cells[x, y + 1, part, :]
            if y > 0:
                moved = moved + low_y * cells[x, y - 1, part, :]
            high, low = split(moved)
            parts[y][0].append(high)
            parts[y][1].append(low)
    for y in range(0, Y, 2):
        stack = [jnp.concatenate(parts[n][0] + parts[n][1], axis=0) for n in (y, y + 1)]
        stack = jnp.concatenate(stack, axis=1)
        out = jnp.dot(
            mix4[...], jnp.concatenate([stack, stack], axis=0), preferred_element_type=F32
        )
        for n in range(2):
            mixed[Y * x + y + n] = out[:, LANES * n : LANES * (n + 1)]


def mix_ends(recv, coef, mix4):
    lane = iota((HALF, LANES), 1)
    ends = jnp.where(lane % 2 == 0, recv[0], pltpu.roll(recv[1], 2, 1))
    ends = jnp.concatenate([ends, pltpu.roll(ends, 64, 1)], axis=0)
    upper = iota((U, LANES), 1) % 2 == 0
    wanted = upper == (coef[SIGN_Z] > 0.5)
    ends = jnp.where(wanted, coef[SPEED_Z] * ends, 0.0)
    return jnp.dot(mix4[...], stacked4(ends), preferred_element_type=F32)


def add_sides(recv, side4, mixed, rows, ways=(0, 1)):
    for way in ways:
        part = pl.ds(HALF * way, HALF)
        for place in range(0, len(rows[way]), 2):
            pair = jnp.concatenate([recv[place, part, :], recv[place + 1, part, :]], axis=1)
            out = jnp.dot(side4[way], stacked4(pair), preferred_element_type=F32)
            for n in range(2):
                row = rows[way][place + n]
                mixed[row] = mixed[row] + out[:, LANES * n : LANES * (n + 1)]


def whole(row, mixed, end_terms):
    lane = iota((U, LANES), 1)
    edge = (lane == 0) | (lane == 127)
    return mixed[row] + jnp.where(edge, pltpu.roll(end_terms, (127 - 2 * row) % 128, 1), 0.0)


def finish(
    mixed, factor, total, forward, sum4, end_terms, out_q, out_density, out_order, q, dens, store_sem
):
    copies = []
    terms = end_terms[...]
    for row in range(ROWS):
        q[row] = factor[row] * whole(row, mixed, terms)
        copy = pltpu.make_async_copy(q.at[row], out_q.at[:, row, 0, :], store_sem.at[row])
        copy.start()
        copies.append(copy)
    for first in range(0, ROWS, 2):
        sums = [
            jnp.concatenate(split(total[row] + forward[row] * q[row]), axis=0)
            for row in (first, first + 1)
        ]
        sums = jnp.concatenate(sums, axis=1)
        summed = jnp.dot(
            sum4[...], jnp.concatenate([sums, sums], axis=0), preferred_element_type=F32
        )
        for n in range(2):
            x, y = divmod(first + n, Y)
            for a in range(4):
                dens[a, x, y : y + 1, :] = summed[a : a + 1, LANES * n : LANES * (n + 1)]
    for copy in (
        pltpu.make_async_copy(dens.at[0], out_density, store_sem.at[ROWS]),
        pltpu.make_async_copy(dens.at[1:4], out_order, store_sem.at[ROWS + 1]),
    ):
        copy.start()
        copies.append(copy)
    for copy in copies:
        copy.wait()


def kernel(
    q_hbm, forward_hbm, iso_hbm, order_hbm, sphere_hbm, sign_hbm, size_hbm, weight_hbm,
    mixed, factor, total, forward_1, sum4, terms_out,
    q, forward_0, field, order, sphere, sign, size, weight,
    cells_0, cells_1, coef, table, mix4, pack, side4,
    send_x, send_y, send_z, recv_x, recv_y, recv_z,
    load_sem, q_sem, forward_sem, send_sem, recv_sem, ready,
):
    forward = (forward_0, forward_1)
    grids = (cells_0, cells_1)
    barrier = pltpu.get_barrier_semaphore()
    here = [lax.axis_index(axis) for axis, _ in SIDES]
    there = [
        lax.rem(index + lax.axis_size(axis) + way, lax.axis_size(axis))
        for index, (axis, way) in zip(here, SIDES)
    ]
    lower = jnp.int32(0)
    for n, (axis, way) in enumerate(SIDES):
        lower = lower + (there[n] < here[n]).astype(jnp.int32)

        @pl.when(there[n] > here[n])
        def _():
            pl.semaphore_signal(
                barrier, inc=1, device_id={axis: there[n]}, device_id_type=pl.DeviceIdType.MESH
            )

    small = [
        pltpu.make_async_copy(src, dst, load_sem.at[n])
        for n, (src, dst) in enumerate(
            [(sign_hbm, sign), (size_hbm, size), (iso_hbm, field), (order_hbm, order),
             (weight_hbm, weight), (sphere_hbm, sphere)]
        )
    ]
    for copy in small:
        copy.start()

    def load_q(row, carry):
        pltpu.make_async_copy(q_hbm.at[:, row, 0, :], q.at[row], q_sem.at[0]).start()
        return carry

    lax.fori_loop(0, ROWS, load_q, 0)

    @pl.when(lower > 0)
    def _():
        pl.semaphore_wait(barrier, lower)

    for n, (axis, way) in enumerate(SIDES):

        @pl.when(there[n] < here[n])
        def _():
            pl.semaphore_signal(
                ready.at[n ^ 1], inc=1, device_id={axis: there[n]}, device_id_type=pl.DeviceIdType.MESH
            )


    small[0].wait()
    small[1].wait()
    signs = sign[...].astype(F32)
    signed = (2.0 * signs - 1.0) * size[...]
    length = jnp.sqrt(jnp.sum(signed * signed, axis=0, keepdims=True))
    along = signed / length
    shape = along * along - 1.0 / 3.0
    speed = 0.5 * jnp.abs(along)
    keep = 1.0 - jnp.sum(speed, axis=0, keepdims=True)
    upper = speed * signs
    lower = speed * (1.0 - signs)
    rows = [
        upper[0:1], lower[0:1], upper[1:2], lower[1:2], speed[2:3], keep,
        RATE * shape[0:1], RATE * shape[1:2], RATE * shape[2:3], signs[2:3],
    ]
    which = iota((16, U), 0)

    def turned(rows):
        stacked = jnp.zeros((16, U), F32)
        for n, row in enumerate(rows):
            stacked = jnp.where(which == n, row, stacked)
        table[:, 0:U] = stacked
        return jnp.transpose(table[...])

    table[...] = jnp.zeros((16, LANES), F32)
    columns = turned(rows)
    for n in (SHAPE_0, SHAPE_1, SHAPE_2):
        coef[n] = jnp.broadcast_to(columns[0:U, n : n + 1], (U, LANES))
    below = (iota((U, U), 0) < iota((U, U), 1)).astype(BF16)
    ones_before = jnp.dot(signs.astype(BF16), below, preferred_element_type=F32)
    place = iota((1, U), 1).astype(F32)
    rank = jnp.where(signs > 0.5, ones_before, HALF + place - ones_before)
    for axis in range(2):
        to_rank = (iota((U, U), 0).astype(F32) == rank[axis : axis + 1]).astype(BF16)
        pack[axis] = jnp.concatenate([to_rank, to_rank], axis=1)

    lane = iota((16, LANES), 1)

    small[2].wait()
    small[3].wait()
    pltpu.make_async_copy(q, q, q_sem.at[0]).wait()
    for x in range(X):
        for group in range(4):
            part = pl.ds(16 * group, 16)
            shapes = [coef[SHAPE_0 + n, part, :] for n in range(3)]
            for y in range(Y):
                exponent = RATE * field[x, y : y + 1, :]
                for n in range(3):
                    exponent = exponent + shapes[n] * order[n, x, y : y + 1, :]
                value = jnp.exp2(exponent)
                factor[Y * x + y, part, :] = value
                cells_0[x, y, part, :] = value * q[Y * x + y, part, :]

    waits = {}
    for step in range(STEPS):
        cells = grids[step]

        def send(n, src, dst):
            axis, way = SIDES[n]
            copy = pltpu.make_async_remote_copy(
                src_ref=src, dst_ref=dst, send_sem=send_sem.at[step, n], recv_sem=recv_sem.at[step, n],
                device_id={axis: there[n]}, device_id_type=pl.DeviceIdType.MESH,
            )
            if step > 0:
                copy.start()
            waits[step, n] = copy
            return copy

        for x in range(X):
            faces = jnp.concatenate([cells[x, 0], cells[x, Y - 1]], axis=1)
            packed = jnp.dot(
                pack[1], jnp.concatenate(split(faces), axis=0), preferred_element_type=F32
            )
            send_y[step, 0, x] = packed[0:HALF, 0:LANES]
            send_y[step, 1, x] = packed[HALF:U, LANES : 2 * LANES]
        come_y = [
            send(2, send_y.at[step, 0], recv_y.at[step, :, 0:HALF, :]),
            send(3, send_y.at[step, 1], recv_y.at[step, :, HALF:U, :]),
        ]
        ends = [jnp.zeros((16, LANES), F32)] * 2
        for x in range(X):
            for group in range(4):
                part = pl.ds(16 * group, 16)
                for y in range(Y):
                    to = 64 * (group // 2) + 2 * (Y * x + y)
                    rolled = pltpu.roll(cells[x, y, part, :], to, 1)
                    chosen = (lane == to) | (lane == (to + 127) % 128)
                    ends[group % 2] = jnp.where(chosen, rolled, ends[group % 2])
        send_z[step, 0:16, :] = ends[0]
        send_z[step, 16:32, :] = ends[1]
        come_z = [
            send(0, send_z.at[step], recv_z.at[step, 0]),
            send(1, send_z.at[step], recv_z.at[step, 1]),
        ]
        for y in range(Y):
            faces = jnp.concatenate([cells[0, y], cells[X - 1, y]], axis=1)
            packed = jnp.dot(
                pack[0], jnp.concatenate(split(faces), axis=0), preferred_element_type=F32
            )
            send_x[step, 0, y] = packed[0:HALF, 0:LANES]
            send_x[step, 1, y] = packed[HALF:U, LANES : 2 * LANES]
        come_x = [
            send(4, send_x.at[step, 0], recv_x.at[step, :, 0:HALF, :]),
            send(5, send_x.at[step, 1], recv_x.at[step, :, HALF:U, :]),
        ]

        if step == 0:
            far = [
                (there[n] > here[n] + 1) | ((there[n] == 2) if axis == "gz" else False)
                for n, (axis, way) in enumerate(SIDES)
            ]
            for n in range(6):
                pl.when(there[n] < here[n])(waits[0, n].start)

            def meet(n):
                pl.semaphore_wait(ready.at[n], 1)
                waits[0, n].start()

            for n in (1, 5, 3, 0, 4, 2):
                pl.when((there[n] > here[n]) & ~far[n])(functools.partial(meet, n))
            for n in (1, 0, 5, 4, 3, 2):
                pl.when((there[n] > here[n]) & far[n])(functools.partial(meet, n))

        if step == 0:
            for n in range(10):
                if n not in (SHAPE_0, SHAPE_1, SHAPE_2):
                    coef[n] = jnp.broadcast_to(columns[0:U, n : n + 1], (U, LANES))
            ranks = turned([rank[0:1], rank[1:2]])

            def load_forward(row, carry):
                for n in range(STEPS):
                    pltpu.make_async_copy(
                        forward_hbm.at[n, :, row, 0, :], forward[n].at[row], forward_sem.at[n]
                    ).start()
                return carry

            lax.fori_loop(0, ROWS, load_forward, 0)
            small[4].wait()
            small[5].wait()
            half_weight = weight[...] / STEPS
            sums = jnp.zeros((16, U), F32)
            for n, row in enumerate(
                [half_weight] + [half_weight * shape[a : a + 1] for a in range(3)]
            ):
                sums = jnp.where(which == n, row, sums)
            high, low = split(sums)
            sum4[...] = jnp.concatenate([high, high, low, low], axis=1)
            high, low = split(sphere[...])
            mix4[...] = jnp.concatenate([high, high, low, low], axis=1)
            for axis in range(2):
                of_rank = ranks[0:U, axis : axis + 1]
                from_rank = (iota((U, U), 1).astype(F32) == of_rank).astype(BF16)
                high, low = split(sphere[...] * speed[axis : axis + 1])
                sorted_mix = jnp.dot(
                    jnp.concatenate([high, low], axis=1),
                    jnp.concatenate([from_rank, from_rank], axis=0),
                    preferred_element_type=F32,
                )
                for way in range(2):
                    high, low = split(sorted_mix[:, HALF * way : HALF * (way + 1)])
                    side4[axis, way] = jnp.concatenate([high, high, low, low], axis=1)

        for x in range(X):
            mix_own(x, cells, coef, mix4, mixed)
        if step == 0:
            for n in range(STEPS):
                pltpu.make_async_copy(forward[n], forward[n], forward_sem.at[n]).wait()

        for copy in come_z:
            copy.wait_recv()
        terms = mix_ends(recv_z.at[step], coef, mix4)
        for copy in come_x:
            copy.wait_recv()
        add_sides(
            recv_x.at[step], side4.at[0], mixed,
            [[Y * (X - 1) + y for y in range(Y)], list(range(Y))],
        )
        def close(ys):
            for row in range(ROWS):
                if row % Y in ys:
                    value = factor[row] * whole(row, mixed, terms)
                    cells_1[row // Y, row % Y] = factor[row] * value
                    total[row] = forward_0[row] * value

        if step == 0:
            close((1, 2))
        for way, copy in enumerate(come_y):
            copy.wait_recv()
            add_sides(
                recv_y.at[step], side4.at[1], mixed,
                [[Y * x + Y - 1 for x in range(X)], [Y * x for x in range(X)]], (way,),
            )
            if step == 0:
                close((Y - 1,) if way == 0 else (0,))
        else:
            terms_out[...] = terms
    for copy in waits.values():
        copy.wait_send()


def body(q_dagger, forward, field_iso, field_order, sphere_step, upwind_sign, direction_size, sphere_weight):
    outside = pl.BlockSpec(memory_space=pltpu.HBM)
    inside = pl.BlockSpec(memory_space=pltpu.VMEM)
    cells = (U, ROWS, 1, LANES)
    block = pltpu.VMEM((ROWS, U, LANES), F32)
    held = pl.pallas_call(
        kernel,
        out_shape=(
            block, block, block, block, pltpu.VMEM((16, 4 * U), BF16), pltpu.VMEM((U, LANES), F32)
        ),
        in_specs=[outside] * 8,
        out_specs=(inside,) * 6,
        scratch_shapes=[
            block,
            block,
            pltpu.VMEM((X, Y, LANES), F32),
            pltpu.VMEM((3, X, Y, LANES), F32),
            pltpu.VMEM((U, U), F32),
            pltpu.VMEM((3, U), jnp.int32),
            pltpu.VMEM((3, U), F32),
            pltpu.VMEM((1, U), F32),
            pltpu.VMEM((X, Y, U, LANES), F32),
            pltpu.VMEM((X, Y, U, LANES), F32),
            pltpu.VMEM((10, U, LANES), F32),
            pltpu.VMEM((16, LANES), F32),
            pltpu.VMEM((U, 4 * U), BF16),
            pltpu.VMEM((2, U, 2 * U), BF16),
            pltpu.VMEM((2, 2, U, LANES), BF16),
            pltpu.VMEM((STEPS, 2, Y, HALF, LANES), F32),
            pltpu.VMEM((STEPS, 2, X, HALF, LANES), F32),
            pltpu.VMEM((STEPS, HALF, LANES), F32),
            pltpu.VMEM((STEPS, Y, U, LANES), F32),
            pltpu.VMEM((STEPS, X, U, LANES), F32),
            pltpu.VMEM((STEPS, 2, HALF, LANES), F32),
            pltpu.SemaphoreType.DMA((6,)),
            pltpu.SemaphoreType.DMA((1,)),
            pltpu.SemaphoreType.DMA((STEPS,)),
            pltpu.SemaphoreType.DMA((STEPS, 6)),
            pltpu.SemaphoreType.DMA((STEPS, 6)),
            pltpu.SemaphoreType.REGULAR((6,)),
        ],
        compiler_params=pltpu.CompilerParams(
            collective_id=0, has_side_effects=True, vmem_limit_bytes=32 * 1024 * 1024
        ),
        name="propagate",
    )(
        *[pltpu.with_memory_space_constraint(array, pltpu.HBM) for array in (
            q_dagger.reshape(cells), forward.reshape((STEPS,) + cells), field_iso, field_order,
            sphere_step, upwind_sign, direction_size, sphere_weight.reshape(1, U),
        )]
    )
    q, density, order = pl.pallas_call(
        finish,
        out_shape=(
            jax.ShapeDtypeStruct(cells, F32),
            jax.ShapeDtypeStruct(field_iso.shape, F32),
            jax.ShapeDtypeStruct(field_order.shape, F32),
        ),
        in_specs=[inside] * 6,
        out_specs=(outside,) * 3,
        scratch_shapes=[
            block,
            pltpu.VMEM((4, X, Y, LANES), F32),
            pltpu.SemaphoreType.DMA((ROWS + 2,)),
        ],
        compiler_params=pltpu.CompilerParams(vmem_limit_bytes=32 * 1024 * 1024),
        name="finish",
    )(*held)
    return q.reshape(q_dagger.shape), density, order


def solution(mesh):
    grid = P("gy", "gx", "gz")
    placed = (
        P(None, "gy", "gx", "gz"), P(None, None, "gy", "gx", "gz"), grid,
        P(None, "gy", "gx", "gz"), P(), P(), P(), P(),
    )
    return jax.shard_map(
        body, mesh=mesh, in_specs=placed,
        out_specs=(P(None, "gy", "gx", "gz"), grid, P(None, "gy", "gx", "gz")), check_vma=False,
    )
```
